128 devices in a mesh: expert: 32 (over y, x, core), fsdp: 4 (over z).
Axes of the slice: x: 4, y: 4, z: 4, core: 2. Of those that a mesh axis runs over, the one named last changes fastest.
Arguments:
- tokens: bfloat16 [32768, 1024], P(('expert', 'fsdp')), may hold values from -6 to 6
- segments: int32 [32768], P(('expert', 'fsdp')), may hold values from 0 to 95, as said below
- positions: int32 [32768], P(('expert', 'fsdp')), may hold values from 0 to 1021, as said below
- routes: int32 [32768, 8], P(('expert', 'fsdp')), may hold values from 0 to 31, all different within a row; in each aligned block of 256 rows (0 to 255, 256 to 511, ...) at most 96 rows name the same one
- w_query: bfloat16 [1024, 1024], P(('expert', 'fsdp')), may hold values from -0.1875 to 0.1875
- w_key: bfloat16 [1024, 512], P(('expert', 'fsdp')), may hold values from -0.1875 to 0.1875
- w_value: bfloat16 [1024, 512], P(('expert', 'fsdp')), may hold values from -0.1875 to 0.1875
- w_output: bfloat16 [1024, 1024], P(('expert', 'fsdp')), may hold values from -1.5 to 1.5
- w_router: bfloat16 [1024, 32], P(('expert', 'fsdp')), may hold values from -0.09375 to 0.09375
- w_gate: bfloat16 [32, 1024, 512], P('expert', 'fsdp'), may hold values from -0.1875 to 0.1875
- w_up: bfloat16 [32, 1024, 512], P('expert', 'fsdp'), may hold values from -0.1875 to 0.1875
- w_down: bfloat16 [32, 512, 1024], P('expert', 'fsdp'), may hold values from -4 to 4
- g_attn: float32 [1024], replicated, may hold values from 0.5 to 1.5
- g_ffn: float32 [1024], replicated, may hold values from 0.5 to 1.5
- g_query: float32 [64], replicated, may hold values from 0.1 to 1.9
- g_key: float32 [64], replicated, may hold values from 0.1 to 1.9
- cotangent: bfloat16 [32768, 1024], P(('expert', 'fsdp')), may hold values from -6 to 6
Outputs:
- output: bfloat16 [32768, 1024], P(('expert', 'fsdp'))
- grad_tokens: bfloat16 [32768, 1024], P(('expert', 'fsdp'))
- grad_query: float32 [1024, 1024], P(('expert', 'fsdp'))
- grad_key: float32 [1024, 512], P(('expert', 'fsdp'))
- grad_value: float32 [1024, 512], P(('expert', 'fsdp'))
- grad_output: float32 [1024, 1024], P(('expert', 'fsdp'))
- grad_router: float32 [1024, 32], P(('expert', 'fsdp'))
- grad_gate: float32 [32, 1024, 512], P('expert', 'fsdp')
- grad_up: float32 [32, 1024, 512], P('expert', 'fsdp')
- grad_down: float32 [32, 512, 1024], P('expert', 'fsdp')
- grad_g_attn: float32 [1024], replicated
- grad_g_ffn: float32 [1024], replicated
- grad_g_query: float32 [64], replicated
- grad_g_key: float32 [64], replicated
The draws below stay inside these ranges and needn't reach their ends.
Inputs may be any that keep to these rules, and one draw needn't show every extreme that they name: `segments`: numbers never fall along the tokens; each sequence of 1024 tokens holds three documents of its own. `positions`: each token's offset from the first token of its document. `routes`: each row names 8 different experts; the 256 rows of one device name no expert more than 96 times, and in some devices' rows some expert exactly 96 times.
All inputs are finite; a program needn't handle non-finite values.
Results may differ from the reference program's by a relative error of at most 0.02.
Values may be sent and summed in bfloat16 or wider, within the bound.
No kernel may reach another device: no remote copies, remote signals or barrier semaphores. Data moves between devices by JAX's collectives and lax.ppermute only.
A program may use at most 192 MiB of HBM per device.

```python
import math
import jax
import jax.numpy as jnp
import numpy as np
from jax import lax

D = 1024
HEADS = 16
KV_HEADS = 8
HEAD = 64
FF = 512
EXPERTS = 32
TOP = 8
TOK_DEV = 256
MOST = 96
SEQ = 1024
TOKENS = 32768


def document_bounds(key):
    count = TOKENS // SEQ
    first = 1 + jax.random.randint(jax.random.fold_in(key, 101), (count, 1), 0, TOK_DEV // 2 - 1)
    last = SEQ - 1 - jax.random.randint(jax.random.fold_in(key, 102), (count, 1), 0, TOK_DEV // 2)
    widest = jax.random.randint(jax.random.fold_in(key, 103), (), 0, count)
    forced = jnp.arange(count, dtype=jnp.int32)[:, None] == widest
    first = jnp.where(forced, 1, first)
    last = jnp.where(forced, SEQ - 1, last)
    index = jnp.arange(SEQ, dtype=jnp.int32)[None, :]
    return (first.astype(jnp.int32), last.astype(jnp.int32), index)


def draw_segments(key, part):
    first, last, index = document_bounds(key)
    count = TOKENS // SEQ
    base = 3 * jnp.arange(count, dtype=jnp.int32)[:, None]
    ids = base + (index >= first).astype(jnp.int32) + (index >= last).astype(jnp.int32)
    return ids.reshape(TOKENS).astype(jnp.int32)


def draw_positions(key, part):
    first, last, index = document_bounds(key)
    start = jnp.where(index >= last, last, jnp.where(index >= first, first, 0))
    return (index - start).reshape(TOKENS).astype(jnp.int32)


def draw_tokens(key, part):
    key = jax.random.fold_in(key, 3)
    values = jax.random.normal(key, (TOKENS, D), jnp.float32)
    return jnp.clip(values, -6.0, 6.0).astype(jnp.bfloat16)


def draw_cotangent(key, part):
    key = jax.random.fold_in(key, 4)
    values = jax.random.normal(key, (TOKENS, D), jnp.float32)
    return jnp.clip(values, -6.0, 6.0).astype(jnp.bfloat16)


def steps_of(key, extent, cuts, low, top_value):
    def one(dim, shards_of):
        steps = jax.random.uniform(jax.random.fold_in(jax.random.fold_in(key, 6), dim), (shards_of,), jnp.float32, low / len(cuts), top_value / len(cuts))
        return jnp.repeat(jnp.exp(steps), extent[dim] // shards_of).reshape((-1,) + (1,) * (len(extent) - dim - 1))

    factor_of = one(*cuts[0])
    for cut in cuts[1:]:
        factor_of = factor_of * one(*cut)
    return factor_of


def assign_block(stream_key, own, number, rows, number_of, top, most, lean):
    ranking = jax.random.permutation(stream_key, number_of)
    packed, ordinary = shares(number_of, rows * top, most, lean, True), shares(number_of, rows * top, most, lean, False)
    places = jnp.arange(number_of)

    def named(sizes, offset_by):
        used = int((sizes > 0).sum())
        fixed = max(1, used // 4)
        moved = fixed + (places - fixed + offset_by * (used - fixed)) % max(1, number_of - fixed)
        return jnp.zeros((number_of,), jnp.int32).at[ranking[jnp.where(places < fixed, places, moved)]].set(jnp.asarray(sizes, jnp.int32))

    sizes = jnp.where(number % 4 == 0, named(packed, number // 4), named(ordinary, number - number // 4 - 1))
    mixed = jax.random.permutation(jax.random.fold_in(own, 3), number_of)
    donor, sink = mixed[0:number_of // 2 * 2:2], mixed[1:number_of // 2 * 2:2]
    slack = jnp.minimum(sizes[donor] - 1, most - sizes[sink]) // 2
    slack = jnp.where((donor == ranking[0]) | (sink == ranking[0]) | (sizes[sink] == 0), 0, jnp.maximum(slack, 0))
    moved = jax.random.randint(jax.random.fold_in(own, 4), (number_of // 2,), 0, 1 << 20) % (slack + 1)
    sizes = sizes.at[donor].add(-moved).at[sink].add(moved)
    members = jnp.searchsorted(jnp.cumsum(sizes), jnp.arange(rows * top), side="right").astype(jnp.int32)
    table = members.reshape(top, rows).T
    table = table[jax.random.permutation(jax.random.fold_in(own, 1), rows)]
    offset_by = jax.random.randint(jax.random.fold_in(own, 2), (rows, 1), 0, top)
    return jnp.take_along_axis(table, (jnp.arange(top)[None, :] + offset_by) % top, axis=1)


def shares(number_of, total, reach, slope, full):
    weights = [(1 << 20) // math.isqrt(grade ** slope) + 1 for grade in range(1, number_of + 1)]
    largest = reach if full else min(reach, max(-(-total // number_of), total * weights[0] // sum(weights)))
    least = 1 if total - largest >= number_of - 1 else 0
    holding, surplus = [largest] + [least] * (number_of - 1), total - largest - least * (number_of - 1)
    while surplus > 0:
        candidates = [i for i in range(1, number_of) if holding[i] < largest] or [i for i in range(1, number_of) if holding[i] < reach]
        pool, remaining = sum([weights[i] for i in candidates]), surplus
        for i in candidates:
            extra = min(reach - holding[i], max(1, remaining * weights[i] // pool), surplus)
            holding[i] = holding[i] + extra
            surplus = surplus - extra
    return np.array(holding)


def gaussian(own_key, extent, spread, limit, shards=(), held_as=jnp.bfloat16):
    drawn = spread * jax.random.normal(own_key, extent, jnp.float32)
    if shards:
        drawn = drawn * steps_of(own_key, extent, shards, -0.22, 0.18)
    return jnp.clip(drawn, -limit, limit).astype(held_as)


def setup_inputs(seed: int = 0) -> dict:
    streams_of = jax.random.split(jax.random.key(seed), 18)
    tokens = draw_tokens(jax.random.fold_in(streams_of[17], 71), 0)
    segments = draw_segments(jax.random.fold_in(streams_of[17], 71), 0)
    positions = draw_positions(jax.random.fold_in(streams_of[17], 71), 0)
    routes_keys = jax.random.split(jax.random.fold_in(streams_of[3], 1), TOKENS // TOK_DEV)
    routes_turns = jax.random.permutation(jax.random.fold_in(streams_of[3], 3), TOKENS // TOK_DEV)
    routes = jax.vmap(lambda own, number: assign_block(jax.random.fold_in(streams_of[3], 2), own, number, TOK_DEV, EXPERTS, TOP, MOST, 1))(routes_keys, routes_turns).reshape((TOKENS, TOP))
    w_query = gaussian(streams_of[4], (D, HEADS * HEAD), D ** -0.5, 0.1875, ((0, 128),))
    w_key = gaussian(streams_of[5], (D, KV_HEADS * HEAD), D ** -0.5, 0.1875, ((0, 128),))
    w_value = gaussian(streams_of[6], (D, KV_HEADS * HEAD), D ** -0.5, 0.1875, ((0, 128),))
    w_output = gaussian(streams_of[7], (HEADS * HEAD, D), (HEADS * HEAD // 64) ** -0.5, 1.5, ((0, 128),))
    w_router = gaussian(streams_of[8], (D, EXPERTS), (4 * D) ** -0.5, 0.09375, ((0, 128),))
    w_gate = gaussian(streams_of[9], (EXPERTS, D, FF), D ** -0.5, 0.1875, ((0, 32), (1, 4)))
    w_up = gaussian(streams_of[10], (EXPERTS, D, FF), D ** -0.5, 0.1875, ((0, 32), (1, 4)))
    w_down = gaussian(streams_of[11], (EXPERTS, FF, D), (max(FF // 256, 1)) ** -0.5, 4.0, ((0, 32), (1, 4)))
    g_attn = jnp.clip(1.0 + 0.1 * jax.random.normal(streams_of[12], (D,), jnp.float32), 0.5, 1.5)
    g_ffn = jnp.clip(1.0 + 0.1 * jax.random.normal(streams_of[13], (D,), jnp.float32), 0.5, 1.5)
    g_query = jnp.clip(1.0 + 0.18 * jax.random.normal(streams_of[14], (HEAD,), jnp.float32), 0.1, 1.9)
    g_key = jnp.clip(1.0 + 0.18 * jax.random.normal(streams_of[15], (HEAD,), jnp.float32), 0.1, 1.9)
    cotangent = draw_cotangent(jax.random.fold_in(streams_of[17], 71), 0)
    return {"tokens": tokens, "segments": segments, "positions": positions, "routes": routes, "w_query": w_query, "w_key": w_key, "w_value": w_value, "w_output": w_output, "w_router": w_router, "w_gate": w_gate, "w_up": w_up, "w_down": w_down, "g_attn": g_attn, "g_ffn": g_ffn, "g_query": g_query, "g_key": g_key, "cotangent": cotangent}


@jax.custom_vjp
def low(v):
    return lax.optimization_barrier(v.astype(jnp.bfloat16)).astype(jnp.float32)

@jax.custom_vjp
def low_back(v):
    return v

def low_keep(v):
    return (low(v), None)

def low_pass(kept, grad):
    return (grad,)

def back_keep(v):
    return (v, None)

def back_low(kept, grad):
    return (low(grad),)
low.defvjp(low_keep, low_pass)
low_back.defvjp(back_keep, back_low)
EPS = 1e-06
NEG = -1e+30
HIGH = lax.Precision.HIGHEST

def matmul(left, right):
    return jnp.dot(left, right, precision=HIGH)

def rms_scale(values, gain):
    return values * lax.rsqrt(lax.optimization_barrier(jnp.mean(values * values, axis=-1, keepdims=True)) + EPS) * gain

def rotate(values, cosine, sine):
    half = values.shape[-1] // 2
    first = values[..., :half]
    second = values[..., half:]
    return jnp.concatenate([first * cosine - second * sine, second * cosine + first * sine], axis=-1)

def rotation(position):
    steps = jnp.arange(HEAD // 2, dtype=jnp.float32)
    freq = jnp.exp(steps * (-2.0 * math.log(10000.0) / HEAD))
    angle = position.astype(jnp.float32)[:, None] * freq[None, :]
    return (jnp.cos(angle)[:, None, :], jnp.sin(angle)[:, None, :])

def prepare_heads(q_raw, k_raw, g_query, g_key, cosine, sine):
    length = q_raw.shape[0]
    queries = rotate(rms_scale(q_raw.reshape(length, -1, HEAD), g_query), cosine, sine)
    keys = rotate(rms_scale(k_raw.reshape(length, -1, HEAD), g_key), cosine, sine)
    return (queries, keys)

def sequence_layer(weights, inputs, segment, position, routes):
    w_query, w_key, w_value, w_output, w_router, w_gate, w_up, w_down, g_attn, g_ffn, g_query, g_key = weights
    length = inputs.shape[0]
    first = low(rms_scale(inputs, g_attn))
    q_raw = low_back(matmul(first, w_query))
    k_raw = low_back(matmul(first, w_key))
    values = low_back(low(matmul(first, w_value))).reshape(length, KV_HEADS, HEAD)
    cosine, sine = rotation(position)
    queries, keys = prepare_heads(q_raw, k_raw, g_query, g_key, cosine, sine)
    queries = low_back(low(queries)).reshape(length, KV_HEADS, HEADS // KV_HEADS, HEAD)
    keys = low_back(low(keys))
    scores = low_back(jnp.einsum('qkgd,skd->kgqs', queries, keys, precision=HIGH) * HEAD ** (-0.5))
    index = jnp.arange(length, dtype=jnp.int32)
    allowed = (segment[:, None] == segment[None, :]) & (index[:, None] >= index[None, :])
    probs = low(jax.nn.softmax(jnp.where(allowed, scores, NEG), axis=-1))
    mixed = jnp.einsum('kgqs,skd->qkgd', probs, values, precision=HIGH).reshape(length, HEADS * HEAD)
    mixed = low_back(low(mixed))
    middle = inputs + low_back(matmul(mixed, w_output))
    second = low(rms_scale(middle, g_ffn))
    logits = low_back(matmul(second, w_router))
    chosen = (routes[:, :, None] == jnp.arange(EXPERTS, dtype=jnp.int32)[None, None, :]).astype(logits.dtype)
    per_expert = lax.optimization_barrier(jnp.sum(chosen, axis=1)) * jax.nn.softmax(logits, axis=-1)
    copies = low_back(jnp.broadcast_to(second, (EXPERTS,) + second.shape))
    gate_pre = low_back(jnp.einsum('eld,edf->elf', copies, w_gate, precision=HIGH))
    up_pre = low_back(jnp.einsum('eld,edf->elf', copies, w_up, precision=HIGH))
    hidden = low_back(low(jax.nn.silu(gate_pre) * up_pre))
    expert_out = low_back(low(jnp.einsum('elf,efd->eld', hidden, w_down, precision=HIGH)))
    return middle + jnp.einsum('le,eld->ld', per_expert, expert_out, precision=HIGH)

def reference(tokens, segments, positions, routes, w_query, w_key, w_value, w_output, w_router, w_gate, w_up, w_down, g_attn, g_ffn, g_query, g_key, cotangent):
    weights = tuple((w.astype(jnp.float32) for w in (w_query, w_key, w_value, w_output, w_router, w_gate, w_up, w_down, g_attn, g_ffn, g_query, g_key)))
    count = TOKENS // SEQ
    layer = jax.checkpoint(sequence_layer)

    def forward(inputs, weights):

        def step(carry, pieces):
            block, segment, position, route = pieces
            return (carry, layer(weights, block, segment, position, route))
        carry, outs = lax.scan(step, (), (inputs.reshape(count, SEQ, D), segments.reshape(count, SEQ), positions.reshape(count, SEQ), routes.reshape(count, SEQ, TOP)))
        return outs.reshape(TOKENS, D)
    result, pullback = jax.vjp(forward, tokens.astype(jnp.float32), weights)
    grad_inputs, grads = pullback(cotangent.astype(jnp.float32))
    return (result.astype(jnp.bfloat16), grad_inputs.astype(jnp.bfloat16), grads[0], grads[1], grads[2], grads[3], grads[4], grads[5], grads[6], grads[7], grads[8], grads[9], grads[10], grads[11])
```

```python
import math

import jax
import jax.numpy as jnp
from jax import lax
from jax.sharding import Mesh, PartitionSpec as P

HEAD = 64
EXPERTS = 32
MOST = 96
EPS = 1e-06
NEG = -1e30
NY, NX, NC, NZ = 4, 4, 2, 4
ALL = ("y", "x", "c", "z")
BF = jnp.bfloat16
F32 = jnp.float32


def mm(a, b):
    return jnp.dot(a, b, preferred_element_type=F32)


def shift(values, axis, step):
    size = lax.axis_size(axis)
    return lax.ppermute(values, axis, [(i, (i + step) % size) for i in range(size)])


def normed(values):
    scale = lax.rsqrt(jnp.mean(values * values, axis=-1, keepdims=True) + EPS)
    return values * scale, scale


def norm_back(grad, unit, scale, gain):
    by_gain = grad * gain
    return scale * (by_gain - unit * jnp.mean(by_gain * unit, axis=-1, keepdims=True))


def rotate(values, cosine, sine):
    half = values.shape[-1] // 2
    first = values[..., :half]
    second = values[..., half:]
    return jnp.concatenate(
        [first * cosine - second * sine, second * cosine + first * sine], axis=-1
    )


def rotation(position):
    steps = jnp.arange(HEAD // 2, dtype=F32)
    freq = jnp.exp(steps * (-2.0 * math.log(10000.0) / HEAD))
    angle = position.astype(F32)[:, None] * freq[None, :]
    return jnp.cos(angle)[:, None, :], jnp.sin(angle)[:, None, :]


def in_order(blocks, place):
    return jnp.take(jnp.stack(blocks), (place - jnp.arange(len(blocks))) % len(blocks), axis=0)


def attention_forward(tokens, position, w_qkv, g_attn, g_query, g_key):
    length = tokens.shape[0]
    unit, _ = normed(tokens.astype(F32))
    first = (unit * g_attn).astype(BF)
    raw = mm(first, w_qkv)
    q_raw = raw[:, :256].reshape(length, 4, HEAD)
    k_raw = raw[:, 256:384].reshape(length, 2, HEAD)
    values = raw[:, 384:].astype(BF).reshape(length, 2, HEAD)
    cosine, sine = rotation(position)
    q_unit, q_scale = normed(q_raw)
    k_unit, k_scale = normed(k_raw)
    queries = rotate(q_unit * g_query, cosine, sine).astype(BF).reshape(length, 2, 2, HEAD)
    keys = rotate(k_unit * g_key, cosine, sine).astype(BF)
    index = jnp.arange(length, dtype=jnp.int32)
    distance = index[:, None] - index[None, :]
    allowed = (distance >= 0) & (distance <= position[:, None])
    scores = jnp.einsum("qkgd,skd->kgqs", queries, keys, preferred_element_type=F32) * HEAD**-0.5
    scores = jnp.where(allowed, scores, NEG)
    largest = jnp.max(scores, axis=-1, keepdims=True)
    log_total = largest + jnp.log(jnp.sum(jnp.exp(scores - largest), axis=-1, keepdims=True))
    probs = jnp.exp(scores - log_total)
    mixed = jnp.einsum("kgqs,skd->qkgd", probs.astype(BF), values, preferred_element_type=F32)
    kept = (unit, first, q_unit, q_scale, k_unit, k_scale, queries, keys, values, probs, cosine, sine)
    return mixed.astype(BF).reshape(length, 256), kept


def attention_backward(grad_mixed, kept, w_qkv, g_query, g_key):
    unit, first, q_unit, q_scale, k_unit, k_scale, queries, keys, values, probs, cosine, sine = kept
    length = grad_mixed.shape[0]
    grad_mixed = grad_mixed.reshape(length, 2, 2, HEAD)
    grad_probs = jnp.einsum("qkgd,skd->kgqs", grad_mixed, values, preferred_element_type=F32)
    delta = jnp.sum(probs * grad_probs, axis=-1, keepdims=True)
    grad_scores = (probs * (grad_probs - delta)).astype(BF)
    scale = HEAD**-0.5
    grad_q = jnp.einsum("kgqs,skd->qkgd", grad_scores, keys, preferred_element_type=F32) * scale
    grad_k = jnp.einsum("kgqs,qkgd->skd", grad_scores, queries, preferred_element_type=F32) * scale
    grad_v = jnp.einsum("kgqs,qkgd->skd", probs.astype(BF), grad_mixed, preferred_element_type=F32)
    grad_q = rotate(grad_q.reshape(length, 4, HEAD).astype(BF).astype(F32), cosine, -sine)
    grad_k = rotate(grad_k.astype(BF).astype(F32), cosine, -sine)
    grad_g_query = jnp.sum(grad_q * q_unit, axis=(0, 1))
    grad_g_key = jnp.sum(grad_k * k_unit, axis=(0, 1))
    grad_q = norm_back(grad_q, q_unit, q_scale, g_query).astype(BF)
    grad_k = norm_back(grad_k, k_unit, k_scale, g_key).astype(BF)
    grad_raw = jnp.concatenate(
        [grad_q.reshape(length, 256), grad_k.reshape(length, 128), grad_v.astype(BF).reshape(length, 128)],
        axis=1,
    )
    grad_first = mm(grad_raw, w_qkv.T)
    grad_w = mm(first.T, grad_raw)
    grad_g_attn = jnp.sum(grad_first * unit, axis=0)
    return grad_first.astype(BF), grad_w.astype(BF), grad_g_attn, grad_g_query, grad_g_key


def pick_rows(routes, expert):
    hit = jnp.any(routes == expert, axis=1)
    rank = jnp.cumsum(hit.astype(jnp.int32)) - 1
    slots = jnp.arange(MOST, dtype=jnp.int32)[:, None]
    return ((rank[None, :] == slots) & hit[None, :]).astype(BF)


def one_expert(second, dout, picks, expert, w_gu, w_down, w_router):
    rows = jnp.concatenate([mm(p, s).astype(BF) for p, s in zip(picks, second)])
    grads = jnp.concatenate([mm(p, g) for p, g in zip(picks, dout)])
    router = jax.nn.softmax(mm(rows, w_router), axis=-1)
    mine = (jnp.arange(EXPERTS, dtype=jnp.int32) == expert).astype(F32)
    gate = jnp.sum(router * mine, axis=-1, keepdims=True)
    both = mm(rows, w_gu)
    gate_pre, up_pre = both[:, :512], both[:, 512:]
    sig = jax.nn.sigmoid(gate_pre)
    silu = gate_pre * sig
    hidden = (silu * up_pre).astype(BF)
    out = mm(hidden, w_down).astype(BF).astype(F32)
    grad_gate = jnp.sum(out * grads, axis=-1, keepdims=True)
    result = (out * gate).astype(BF)
    dy = (grads * gate).astype(BF)
    grad_hidden = mm(dy, w_down.T).astype(BF).astype(F32)
    grad_gp = (grad_hidden * up_pre * sig * (1.0 + gate_pre * (1.0 - sig))).astype(BF)
    grad_up = (grad_hidden * silu).astype(BF)
    grad_both = jnp.concatenate([grad_gp, grad_up], axis=1)
    grad_logits = (router * (mine - gate) * grad_gate).astype(BF)
    back = (mm(grad_both, w_gu.T) + mm(grad_logits, w_router.T)).astype(BF)
    grad_w_gu = mm(rows.T, grad_both).astype(BF)
    grad_w_down = mm(hidden.T, dy).astype(BF)
    grad_w_router = mm(rows.T, grad_logits)
    return result, back, grad_w_gu, grad_w_down, grad_w_router


def spread_rows(values):
    own_x = [values] + [shift(values, "y", k) for k in range(1, NY)]
    return own_x + [shift(v, "c", 1) for v in own_x]


def collect_rows(blocks):
    over = [shift(b, "c", 1) for b in blocks[NY:]]
    mine = [(a.astype(F32) + b.astype(F32)).astype(BF) for a, b in zip(blocks[:NY], over)]
    back = [mine[0]] + [shift(mine[k], "y", -k) for k in range(1, NY)]
    total = back[0].astype(F32)
    for b in back[1:]:
        total = total + b.astype(F32)
    return total


def add_up(blocks):
    total = blocks[0].astype(F32)
    for b in blocks[1:]:
        total = total + b.astype(F32)
    return total


def block_of(values, place, size):
    return lax.dynamic_slice_in_dim(values, (place % NZ) * size, size, axis=0)


def per_device(
    tokens,
    segments,
    positions,
    routes,
    w_query,
    w_key,
    w_value,
    w_output,
    w_router,
    w_gate,
    w_up,
    w_down,
    g_attn,
    g_ffn,
    g_query,
    g_key,
    cotangent,
):
    y, x, c, z = (lax.axis_index(a) for a in ALL)
    devices = NY * NX * NC * NZ

    token_parts = [tokens] + [shift(tokens, "z", k) for k in range(1, NZ)]
    position_parts = [positions] + [shift(positions, "z", k) for k in range(1, NZ)]
    by_head = jnp.concatenate(
        [w_query.reshape(8, NZ, 256), w_key.reshape(8, NZ, 128), w_value.reshape(8, NZ, 128)], axis=2
    ).transpose(1, 0, 2)
    w_qkv = lax.all_to_all(
        jnp.broadcast_to(by_head[None], (devices // NZ, NZ, 8, 512)).reshape(devices, 8, 512), ALL, 0, 0
    ).reshape(1024, 512)
    out_router = lax.all_gather(jnp.concatenate([w_output, w_router], axis=1), ALL, axis=0, tiled=True)
    w_out, w_rout = out_router[:, :1024], out_router[:, 1024:]
    dout = spread_rows(cotangent)
    routes_all = spread_rows(routes)
    gu_own = jnp.concatenate([w_gate[0], w_up[0]], axis=1)
    gu_z = jnp.stack([gu_own] + [shift(gu_own, "z", k) for k in range(1, NZ)])
    gu = [gu_z] + [shift(gu_z, "x", j) for j in range(1, NX)]
    down_own = w_down[0]
    down_x = jnp.stack([down_own] + [shift(down_own, "x", j) for j in range(1, NX)])
    down = [down_x] + [shift(down_x, "z", k) for k in range(1, NZ)]

    sequence = in_order(token_parts, z).reshape(1024, 1024)
    position = in_order(position_parts, z).reshape(1024)
    mixed_heads, kept = attention_forward(sequence, position, w_qkv, g_attn, g_query, g_key)
    mixed = (
        lax.all_to_all(mixed_heads.reshape(NZ, 256, 256), "z", 0, 0).transpose(1, 0, 2).reshape(256, 1024)
    )
    middle = tokens.astype(F32) + mm(mixed, w_out)
    unit, scale = normed(middle)
    second = spread_rows((unit * g_ffn).astype(BF))

    results, backs, picks = [], [], []
    grads_gu, grads_down = [], []
    grad_router = 0.0
    for j in range(NX):
        expert = (y * NX + (x - j) % NX) * NC + c
        w_gu = in_order([gu[j][k] for k in range(NZ)], z).reshape(1024, 1024)
        w_dn = in_order([down[k][j] for k in range(NZ)], z).reshape(512, 1024)
        pick = [pick_rows(r, expert) for r in routes_all]
        result, back, grad_gu, grad_dn, grad_r = one_expert(second, dout, pick, expert, w_gu, w_dn, w_rout)
        results.append(result.reshape(8, MOST, 1024))
        backs.append(back.reshape(8, MOST, 1024))
        picks.append(pick)
        grads_gu.append(grad_gu)
        grads_down.append(grad_dn)
        grad_router = grad_router + grad_r
    picks = [jnp.concatenate([picks[j][b] for j in range(NX)]) for b in range(8)]

    def to_tokens(rows):
        return [mm(picks[b].T, jnp.concatenate([r[b] for r in rows])).astype(BF) for b in range(8)]

    grad_second = collect_rows(to_tokens(backs))
    mixture = collect_rows(to_tokens(results))
    output = (middle + mixture).astype(BF)

    grad_out = cotangent.astype(F32)
    grad_middle = grad_out + norm_back(grad_second, unit, scale, g_ffn)
    grad_g_ffn = jnp.sum(grad_second * unit, axis=0)
    da = grad_middle.astype(BF)
    grad_out_w = jnp.concatenate([mm(mixed.T, da), grad_router], axis=1).astype(BF)
    grad_out_parts = lax.all_to_all(grad_out_w.reshape(devices, 8, 1056), ALL, 0, 0)
    dense = jnp.sum(grad_out_parts.astype(F32), axis=0)
    grad_mixed = mm(da, w_out.T).astype(BF)
    grad_heads = lax.all_to_all(grad_mixed.reshape(256, NZ, 256).transpose(1, 0, 2), "z", 0, 0).reshape(
        1024, 256
    )
    grad_first, grad_w, grad_g_attn, grad_g_query, grad_g_key = attention_backward(
        grad_heads, kept, w_qkv, g_query, g_key
    )
    grad_first = jnp.sum(
        lax.all_to_all(grad_first.reshape(NZ, 256, 1024), "z", 0, 0).astype(F32), axis=0
    )
    unit_first, scale_first = normed(tokens.astype(F32))
    grad_tokens = (grad_middle + norm_back(grad_first, unit_first, scale_first, g_attn)).astype(BF)

    grad_w = lax.all_to_all(grad_w.reshape(devices, 8, 512), ALL, 0, 0)
    grad_w = jnp.sum(grad_w.astype(F32).reshape(devices // NZ, NZ, 8, 512), axis=0)
    grad_query = grad_w[:, :, :256].transpose(1, 0, 2).reshape(8, 1024)
    grad_key = grad_w[:, :, 256:384].transpose(1, 0, 2).reshape(8, 512)
    grad_value = grad_w[:, :, 384:].transpose(1, 0, 2).reshape(8, 512)
    gains = jnp.concatenate([grad_g_attn, grad_g_ffn, grad_g_query, grad_g_key]).reshape(1, 17, 128)
    gains = lax.all_to_all(jnp.broadcast_to(gains, (devices, 17, 128)), ALL, 0, 0)
    gains = jnp.sum(gains, axis=0).reshape(17 * 128)

    grad_gu = add_up([grads_gu[0]] + [shift(grads_gu[j], "x", -j) for j in range(1, NX)]).astype(BF)
    grad_gu = add_up(
        [block_of(grad_gu, z, 256)] + [shift(block_of(grad_gu, z + k, 256), "z", k) for k in range(1, NZ)]
    )
    stacked = jnp.concatenate(grads_down, axis=1)
    grad_dn = add_up(
        [block_of(stacked, z, 128)] + [shift(block_of(stacked, z + k, 128), "z", k) for k in range(1, NZ)]
    ).astype(BF)
    grad_dn = add_up(
        [grad_dn[:, :1024]]
        + [shift(grad_dn[:, 1024 * j : 1024 * (j + 1)], "x", -j) for j in range(1, NX)]
    )
    return (
        output,
        grad_tokens,
        grad_query,
        grad_key,
        grad_value,
        dense[:, :1024],
        dense[:, 1024:],
        grad_gu[None, :, :512],
        grad_gu[None, :, 512:],
        grad_dn[None],
        gains[:1024],
        gains[1024:2048],
        gains[2048:2112],
        gains[2112:2176],
    )


def solution(mesh):
    grid = Mesh(mesh.devices.reshape(NY, NX, NC, NZ), ALL)
    rows = P(ALL, None)
    line = P(ALL)
    expert = P(("y", "x", "c"), "z", None)
    in_specs = (rows, line, line, rows) + (rows,) * 5 + (expert,) * 3 + (P(),) * 4 + (rows,)
    out_specs = (rows,) * 7 + (expert,) * 3 + (P(),) * 4
    return jax.shard_map(
        per_device, mesh=grid, in_specs=in_specs, out_specs=out_specs, check_vma=False
    )
```

```python
import math
from functools import partial

import jax
import jax.numpy as jnp
from jax import lax
from jax.experimental import pallas as pl
from jax.experimental.pallas import tpu as pltpu
from jax.sharding import Mesh, PartitionSpec as P

HEAD = 64
EXPERTS = 32
MOST = 96
EPS = 1e-06
NEG = -1e30
NY, NX, NC, NZ = 4, 4, 2, 4
ALL = ("y", "x", "c", "z")
SAME_CORE = ("y", "x", "z")
BLOCKS = NY * NC
ROWS = BLOCKS * MOST
BF = jnp.bfloat16
F32 = jnp.float32
VMEM_LIMIT = 60 * 1024 * 1024
COST = pl.CostEstimate(flops=1000, bytes_accessed=1000, transcendentals=0)


def mm(a, b):
    return jnp.dot(a, b, preferred_element_type=F32)


def mm_nt(a, b):
    return lax.dot_general(a, b, (((1,), (1,)), ((), ())), preferred_element_type=F32)


def mm_tn(a, b):
    return lax.dot_general(a, b, (((0,), (0,)), ((), ())), preferred_element_type=F32)


def call(body, out_shape, place, *args, scratch=(), cost=None):
    whole = pl.BlockSpec(memory_space=pltpu.VMEM)
    return pl.pallas_call(
        body,
        out_shape=out_shape,
        in_specs=[pl.BlockSpec(memory_space=pltpu.SMEM)] + [whole] * len(args),
        out_specs=[whole] * len(out_shape),
        scratch_shapes=list(scratch),
        compiler_params=pltpu.CompilerParams(vmem_limit_bytes=VMEM_LIMIT),
        cost_estimate=cost,
    )(place, *args)


def shaped(shape, dtype):
    return jax.ShapeDtypeStruct(shape, dtype)


def halves_swapped(values):
    width = values.shape[1]
    lane = lax.broadcasted_iota(jnp.int32, values.shape, 1)
    low = (lane % HEAD) < (HEAD // 2)
    return jnp.where(
        low, pltpu.roll(values, width - HEAD // 2, 1), pltpu.roll(values, HEAD // 2, 1)
    )


def head_mean(values):
    width = values.shape[1]
    row = lax.broadcasted_iota(jnp.int32, (width, width), 0) // HEAD
    col = lax.broadcasted_iota(jnp.int32, (width, width), 1) // HEAD
    ones = jnp.where(row == col, 1.0 / HEAD, 0.0).astype(BF)
    high = values.astype(BF)
    rest = (values - high.astype(F32)).astype(BF)
    return mm(high, ones) + mm(rest, ones)


def unit_rows(values):
    scale = lax.rsqrt(jnp.mean(values * values, axis=-1, keepdims=True) + EPS)
    return values * scale, scale


def wide(values, width):
    return jnp.concatenate([values] * (width // values.shape[1]), axis=1)


def block_rows(place):
    return pl.ds(pl.multiple_of(lax.rem(place + NZ, NZ) * 256, 256), 256)


def both_cores(to_ref, near_ref, far_ref, c, width):
    for n in range(NY * NX):
        for src, core in ((near_ref, c), (far_ref, 1 - c)):
            to_ref[pl.ds(pl.multiple_of(n * 64 + core * 32, 32), 32), :] = src[n * 32 : (n + 1) * 32, :width]


def each_core(near_ref, far_ref, src_ref, c):
    for n in range(NY * NX):
        for dst, core in ((near_ref, c), (far_ref, 1 - c)):
            dst[n * 32 : (n + 1) * 32, :] = src_ref[pl.ds(pl.multiple_of(n * 64 + core * 32, 32), 32), :]


def for_each(values):
    width = values.shape[1]
    rows = [values[:, k * 128 : (k + 1) * 128] for k in range(width // 128)]
    rows = rows + [jnp.zeros((1, 128), F32)] * (8 - len(rows))
    rows = jnp.concatenate(rows, axis=0)
    return jnp.broadcast_to(rows[None], (128, 8, 128)).reshape(1024, 128).astype(BF)


def key_mask(positions_ref, i):
    keys = (i + 1) * 256
    key = lax.broadcasted_iota(jnp.int32, (keys, 256), 0)
    query = i * 256 + lax.broadcasted_iota(jnp.int32, (1, 256), 1)
    first = query - positions_ref[:, i * 256 : (i + 1) * 256]
    return (key >= first) & (key <= query)


def attention_forward_kernel(
    place_ref, t0, t1, t2, t3, near_ref, far_ref, ga_ref, gq_ref, gk_ref,
    m0, m1, m2, m3, seq_ref, w_ref, pos_ref, cos_ref, sin_ref, raw_ref, q_ref, k_ref, v_ref, lse_ref,
    vt_ref, mixed_ref,
):
    z, c = place_ref[2], place_ref[3]
    both_cores(w_ref, near_ref, far_ref, c, 512)
    at = (place_ref[1] * NX + place_ref[0]) * 32
    packed = near_ref[pl.ds(pl.multiple_of(at, 32), 32), 512:].astype(F32)
    packed = [packed[8 * k + r : 8 * k + r + 1] * 32.0 + packed[8 * k + r + 2 : 8 * k + r + 3] for k in range(NZ) for r in range(2)]
    position = jnp.concatenate(packed, axis=1)
    pos_ref[...] = position.astype(jnp.int32)
    step = lax.broadcasted_iota(jnp.int32, (HEAD // 2, 1024), 0).astype(F32)
    angle = jnp.exp(step * (-2.0 * math.log(10000.0) / HEAD)) * position
    cos, sin = jnp.cos(angle).T, jnp.sin(angle).T
    cos_ref[...] = jnp.concatenate([cos] * 4, axis=1)
    sin_ref[...] = jnp.concatenate([-sin, sin] * 2, axis=1)
    for k, tokens_ref in enumerate((t0, t1, t2, t3)):
        seq_ref[block_rows(z - k), :] = tokens_ref[...]

    def project(i, _):
        rows = pl.ds(pl.multiple_of(i * 256, 256), 256)
        unit, _ = unit_rows(seq_ref[rows, :].astype(F32))
        raw = mm((unit * ga_ref[...]).astype(BF), w_ref[...])
        raw_ref[rows, :] = raw[:, :384]
        cos, sin = cos_ref[rows, :], sin_ref[rows, :]
        for width, start, gain_ref, out_ref in ((256, 0, gq_ref, q_ref), (128, 256, gk_ref, k_ref)):
            part = raw[:, start : start + width]
            part = part * lax.rsqrt(head_mean(part * part) + EPS) * wide(gain_ref[...], width)
            part = part * wide(cos, width) + halves_swapped(part) * wide(sin, width)
            part = part.astype(BF)
            for h in range(width // HEAD):
                out_ref[h, rows, :] = part[:, h * HEAD : (h + 1) * HEAD]
        values = raw[:, 384:].astype(BF)
        for h in range(2):
            v_ref[h, rows, :] = values[:, h * HEAD : (h + 1) * HEAD]
        vt_ref[:, rows] = values.astype(F32).T.astype(BF)
        return 0

    lax.fori_loop(0, 4, project, 0)
    for i in range(4):
        keys = (i + 1) * 256
        allowed = key_mask(pos_ref, i)

        def pair(g, _, i=i, keys=keys, allowed=allowed):
            outs = []
            for s in range(2):
                scores = mm_nt(k_ref[g, :keys, :], q_ref[2 * g + s, i * 256 : keys, :]) * HEAD**-0.5
                scores = jnp.where(allowed, scores, NEG)
                top = jnp.max(scores, axis=0, keepdims=True)
                probs = jnp.exp(scores - top)
                total = jnp.sum(probs, axis=0, keepdims=True)
                lse_ref[2 * g + s, :, i * 256 : keys] = top + jnp.log(total)
                at = pl.ds(pl.multiple_of(g * HEAD, HEAD), HEAD)
                outs.append(mm(vt_ref[at, :keys], probs.astype(BF)) / total)
            both = jnp.concatenate(outs, axis=0).T
            mixed_ref[i * 256 : keys, pl.ds(pl.multiple_of(g * 128, 128), 128)] = both.astype(BF)
            return 0

        lax.fori_loop(0, 2, pair, 0)
    for k, out_ref in enumerate((m0, m1, m2, m3)):
        out_ref[...] = mixed_ref[block_rows(z + k), :]


def attention_forward(place, tokens, near, far, g_attn, g_query, g_key):
    return call(
        attention_forward_kernel,
        [shaped((256, 256), BF)] * NZ + [
            shaped((1024, 1024), BF), shaped((1024, 512), BF), shaped((1, 1024), jnp.int32),
            shaped((1024, 128), F32), shaped((1024, 128), F32), shaped((1024, 384), F32), shaped((4, 1024, HEAD), BF),
            shaped((2, 1024, HEAD), BF), shaped((2, 1024, HEAD), BF), shaped((4, 1, 1024), F32),
        ],
        place, *tokens, near, far, g_attn, g_query, g_key,
        scratch=[pltpu.VMEM((128, 1024), BF), pltpu.VMEM((1024, 256), BF)],
        cost=COST,
    )


def attention_backward_kernel(
    place_ref, gm0, gm1, gm2, gm3, ga_ref, gq_ref, gk_ref,
    seq_ref, w_ref, pos_ref, cos_ref, sin_ref, raw_ref, q_ref, k_ref, v_ref, lse_ref,
    gf0, gf1, gf2, gf3, near_ref, far_ref,
    gw_ref, kt_ref, do_ref, dq_ref, dk_ref, dv_ref, first_ref, graw_ref, gains_ref, heads_ref,
):
    z = place_ref[2]
    for h in range(4):
        for k, gm_ref in enumerate((gm0, gm1, gm2, gm3)):
            do_ref[h, block_rows(z - k), :] = gm_ref[:, h * HEAD : (h + 1) * HEAD]
    for g in range(2):
        kt_ref[g] = k_ref[g].astype(F32).T.astype(BF)
        dk_ref[g] = jnp.zeros((1024, HEAD), F32)
        dv_ref[g] = jnp.zeros((1024, HEAD), F32)
    for i in range(4):
        keys = (i + 1) * 256
        rows = slice(i * 256, keys)
        allowed = key_mask(pos_ref, i)

        def pair(g, _, keys=keys, rows=rows, allowed=allowed):
            grads = []
            dk = jnp.zeros((keys, HEAD), F32)
            dv = jnp.zeros((keys, HEAD), F32)
            for s in range(2):
                h = 2 * g + s
                query, dout = q_ref[h, rows, :], do_ref[h, rows, :]
                scores = mm_nt(k_ref[g, :keys, :], query) * HEAD**-0.5
                probs = jnp.where(allowed, jnp.exp(scores - lse_ref[h, :, rows]), 0.0)
                grad_probs = mm_nt(v_ref[g, :keys, :], dout)
                delta = jnp.sum(probs * grad_probs, axis=0, keepdims=True)
                grad_scores = (probs * (grad_probs - delta)).astype(BF)
                dv = dv + mm(probs.astype(BF), dout)
                dk = dk + mm(grad_scores, query)
                grads.append(mm(kt_ref[g, :, :keys], grad_scores) * HEAD**-0.5)
            dk_ref[g, :keys, :] += dk
            dv_ref[g, :keys, :] += dv
            both = jnp.concatenate(grads, axis=0).T
            dq_ref[rows, pl.ds(pl.multiple_of(g * 128, 128), 128)] = both
            return 0

        lax.fori_loop(0, 2, pair, 0)

    gains_ref[...] = jnp.zeros((1, 1024), F32)
    heads_ref[...] = jnp.zeros((1, 384), F32)

    for k, gf_ref in enumerate((gf0, gf1, gf2, gf3)):
        rows = block_rows(z + k)
        cos, sin = cos_ref[rows, :], sin_ref[rows, :]
        dk = jnp.concatenate([dk_ref[0, rows, :], dk_ref[1, rows, :]], axis=1) * HEAD**-0.5
        dv = jnp.concatenate([dv_ref[0, rows, :], dv_ref[1, rows, :]], axis=1)
        for width, start, gain_ref, grad in (
            (256, 0, gq_ref, dq_ref[rows, :]),
            (128, 256, gk_ref, dk),
        ):
            grad = grad.astype(BF).astype(F32)
            grad = grad * wide(cos, width) - halves_swapped(grad) * wide(sin, width)
            part = raw_ref[rows, start : start + width]
            scale = lax.rsqrt(head_mean(part * part) + EPS)
            part = part * scale
            heads_ref[:, start : start + width] += jnp.sum(grad * part, axis=0, keepdims=True)
            grad = grad * wide(gain_ref[...], width)
            grad = scale * (grad - part * head_mean(grad * part))
            graw_ref[rows, start : start + width] = grad.astype(BF)
        graw_ref[rows, 384:] = dv.astype(BF)
        unit, _ = unit_rows(seq_ref[rows, :].astype(F32))
        first_ref[rows, :] = (unit * ga_ref[...]).astype(BF)
        grad_first = mm_nt(graw_ref[rows, :], w_ref[...])
        gains_ref[...] += jnp.sum(grad_first * unit, axis=0, keepdims=True)
        gf_ref[...] = grad_first.astype(BF)

    def weights(i, _):
        rows = pl.ds(pl.multiple_of(i * 256, 256), 256)
        gw_ref[rows, :512] = mm_tn(first_ref[:, rows], graw_ref[...]).astype(BF)
        return 0

    lax.fori_loop(0, 4, weights, 0)
    gw_ref[:, 512:640] = for_each(gains_ref[...])
    gw_ref[:, 640:] = for_each(heads_ref[...])
    each_core(near_ref, far_ref, gw_ref, place_ref[3])


def attention_backward(place, grad_mixed, g_attn, g_query, g_key, kept):
    return call(
        attention_backward_kernel,
        [shaped((256, 1024), BF)] * NZ + [shaped((512, 768), BF)] * 2,
        place, *grad_mixed, g_attn, g_query, g_key, *kept,
        scratch=[
            pltpu.VMEM((1024, 768), BF),
            pltpu.VMEM((2, HEAD, 1024), BF), pltpu.VMEM((4, 1024, HEAD), BF), pltpu.VMEM((1024, 256), F32),
            pltpu.VMEM((2, 1024, HEAD), F32), pltpu.VMEM((2, 1024, HEAD), F32), pltpu.VMEM((1024, 1024), BF),
            pltpu.VMEM((1024, 512), BF), pltpu.VMEM((1, 1024), F32), pltpu.VMEM((1, 384), F32),
        ],
        cost=COST,
    )


def middle_kernel(
    place_ref, tokens_ref, m0, m1, m2, m3, near_ref, far_ref, g_ref,
    middle_ref, second_ref, w_ref, router_ref, all_ref,
):
    z = place_ref[2]
    both_cores(all_ref, near_ref, far_ref, place_ref[3], 1152)
    w_ref[...] = all_ref[:, :1024]
    router_ref[...] = all_ref[:, 1024:]
    total = tokens_ref[...].astype(F32)
    for k, mixed_ref in enumerate((m0, m1, m2, m3)):
        total = total + mm(mixed_ref[...], w_ref[block_rows(z - k), :])
    middle_ref[...] = total
    unit, _ = unit_rows(total)
    second = (unit * g_ref[...]).astype(BF)
    for k in range(NY):
        second_ref[k] = second


def middle_step(place, tokens, mixed, near, far, g_ffn):
    return call(
        middle_kernel,
        [
            shaped((256, 1024), F32), shaped((NY, 256, 1024), BF), shaped((1024, 1024), BF),
            shaped((1024, 128), BF),
        ],
        place, tokens, *mixed, near, far, g_ffn,
        scratch=[pltpu.VMEM((1024, 1152), BF)],
        cost=COST,
    )


def middle_back_kernel(
    place_ref, b0, b1, b2, b3, middle_ref, dout_ref, w_ref, g_ref,
    grad_ref, gm0, gm1, gm2, gm3, da_ref, gain_ref,
):
    z = place_ref[2]
    grad = b0[...].astype(F32)
    for back_ref in (b1, b2, b3):
        grad = grad + back_ref[...].astype(F32)
    unit, scale = unit_rows(middle_ref[...])
    gain_ref[...] = jnp.sum(grad * unit, axis=0, keepdims=True)
    grad = grad * g_ref[...]
    grad = dout_ref[...].astype(F32) + scale * (grad - unit * jnp.mean(grad * unit, axis=-1, keepdims=True))
    grad_ref[...] = grad
    da_ref[...] = grad.astype(BF)
    for k, gm_ref in enumerate((gm0, gm1, gm2, gm3)):
        gm_ref[...] = mm_nt(da_ref[...], w_ref[block_rows(z + k), :]).astype(BF)


def middle_back(place, back, middle, dout, w_out, g_ffn):
    return call(
        middle_back_kernel,
        [
            shaped((256, 1024), F32), *[shaped((256, 256), BF)] * NZ, shaped((256, 1024), BF),
            shaped((1, 1024), F32),
        ],
        place, *back, middle, dout, w_out, g_ffn,
        cost=COST,
    )


def output_weight_kernel(
    place_ref, da_ref, m0, m1, m2, m3, router_ref, gain_ref, near_ref, far_ref, gw_ref,
):
    z = place_ref[2]
    for k, mixed_ref in enumerate((m0, m1, m2, m3)):
        gw_ref[block_rows(z - k), :1024] = mm_tn(mixed_ref[...], da_ref[...]).astype(BF)
    gw_ref[:, 1024:1152] = router_ref[...].astype(BF)
    gw_ref[:, 1152:] = for_each(gain_ref[...])
    each_core(near_ref, far_ref, gw_ref, place_ref[3])


def output_weight(place, da, mixed, grad_router, gain):
    return call(
        output_weight_kernel,
        [shaped((512, 1280), BF)] * 2,
        place, da, *mixed, grad_router, gain,
        scratch=[pltpu.VMEM((1024, 1280), BF)],
        cost=COST,
    )


def find_rows(routes, expert):
    hits = [
        jnp.sum(jnp.where(routes[b] == expert.astype(F32), 1.0, 0.0), axis=0, keepdims=True)
        for b in range(BLOCKS)
    ]
    hits = jnp.concatenate(hits, axis=0)
    row = lax.broadcasted_iota(jnp.int32, (256, 256), 0)
    before = jnp.where(row < lax.broadcasted_iota(jnp.int32, (256, 256), 1), 1.0, 0.0).astype(BF)
    rank = mm(hits.astype(BF), before)
    slots = lax.broadcasted_iota(jnp.int32, (MOST, 256), 0).astype(F32)
    return [
        jnp.where((rank[b : b + 1, :] == slots) & (hits[b : b + 1, :] > 0.5), 1.0, 0.0).astype(BF)
        for b in range(BLOCKS)
    ]


def one_expert(picks, expert, second, dout, wr_ref, gu, dn, wait, rows, grads, pre, hidden, dy, both, logit_grad,
               put_result, put_back, gw_ref, gwr_ref):
    for b in range(BLOCKS):
        at = slice(b * MOST, (b + 1) * MOST)
        rows[at, :] = mm(picks[b], second[b]).astype(BF)
        grads[at, :] = mm(picks[b], dout[b, :, :1024]).astype(BF)
    logits = mm(rows[...], wr_ref[...])
    lane = lax.broadcasted_iota(jnp.int32, (ROWS, 128), 1)
    logits = jnp.where(lane < EXPERTS, logits, NEG)
    router = jnp.exp(logits - jnp.max(logits, axis=-1, keepdims=True))
    router = router / jnp.sum(router, axis=-1, keepdims=True)
    mine = jnp.where(lane == expert, 1.0, 0.0)
    gate = jnp.sum(router * mine, axis=-1, keepdims=True)
    wait()
    for f in range(2):
        g_at, u_at = slice(f * 256, (f + 1) * 256), slice(512 + f * 256, 768 + f * 256)
        gate_pre = mm(rows[...], gu[:, g_at])
        up_pre = mm(rows[...], gu[:, u_at])
        pre[:, g_at] = gate_pre
        pre[:, u_at] = up_pre
        hidden[:, g_at] = (gate_pre * jax.nn.sigmoid(gate_pre) * up_pre).astype(BF)
    grad_gate = jnp.zeros((ROWS, 1), F32)
    for d in range(4):
        at = slice(d * 256, (d + 1) * 256)
        out = mm(hidden[...], dn[:, at]).astype(BF).astype(F32)
        grad = grads[:, at].astype(F32)
        grad_gate = grad_gate + jnp.sum(out * grad, axis=-1, keepdims=True)
        put_result(at, (out * gate).astype(BF))
        dy[:, at] = (grad * gate).astype(BF)
    logit_grad[...] = (router * (mine - gate) * grad_gate).astype(BF)
    for f in range(2):
        g_at, u_at = slice(f * 256, (f + 1) * 256), slice(512 + f * 256, 768 + f * 256)
        grad_hidden = mm_nt(dy[...], dn[g_at, :]).astype(BF).astype(F32)
        gate_pre, up_pre = pre[:, g_at], pre[:, u_at]
        sig = jax.nn.sigmoid(gate_pre)
        both[:, g_at] = (grad_hidden * up_pre * sig * (1.0 + gate_pre * (1.0 - sig))).astype(BF)
        both[:, u_at] = (grad_hidden * (gate_pre * sig)).astype(BF)
    for d in range(4):
        at = slice(d * 256, (d + 1) * 256)
        put_back(at, (mm_nt(both[...], gu[at, :]) + mm_nt(logit_grad[...], wr_ref[at, :])).astype(BF))
        gw_ref[0, d, :256, :] = mm_tn(rows[:, at], both[...]).astype(BF)
        gwr_ref[at, :] += mm_tn(rows[:, at], logit_grad[...])
    for f in range(2):
        at = slice(f * 256, (f + 1) * 256)
        grad = mm_tn(hidden[:, at], dy[...]).astype(BF)
        gw_ref[0, 2 * f, 256:, :] = grad[:128]
        gw_ref[0, 2 * f + 1, 256:, :] = grad[128:]


def experts_kernel(
    place_ref, wr_ref, w_ref, s0_ref, s1_ref, d0_ref, d1_ref,
    back0, back1, res0, res1, gw_ref, gwr_ref,
    second, dout, gu_w, dn_w, rows, grads, pre, hidden, dy, both, logit_grad, routes, picks, results, backs, stage,
    in_sems, w_sems, out_sems,
):
    j = pl.program_id(0)
    y, c = place_ref[1], place_ref[3]
    def weight_copies(n):
        slot = n % 2
        copies = []
        for q in range(NZ):
            gu, dn = w_ref.at[n, q, pl.ds(0, 256)], w_ref.at[n, q, pl.ds(256, 128)]
            copies.append(pltpu.make_async_copy(gu, gu_w.at[slot, pl.ds(q * 256, 256)], w_sems.at[slot, q]))
            copies.append(pltpu.make_async_copy(dn, dn_w.at[slot, pl.ds(q * 128, 128)], w_sems.at[slot, NZ + q]))
        return copies

    copies = [
        pltpu.make_async_copy(s0_ref, second.at[pl.ds(0, NY)], in_sems.at[0]),
        pltpu.make_async_copy(s1_ref, second.at[pl.ds(NY, NY)], in_sems.at[1]),
    ]
    for n in range(BLOCKS):
        to = (n // NY) * NY + lax.rem(y - n % NY + NY, NY)
        src = (d0_ref, d1_ref)[n // NY].at[n % NY]
        copies.append(pltpu.make_async_copy(src, dout.at[to], in_sems.at[2 + n]))

    @pl.when(j == 0)
    def _():
        for copy in copies + weight_copies(0):
            copy.start()
        gwr_ref[...] = jnp.zeros_like(gwr_ref)
        for copy in copies:
            copy.wait()
        for b in range(BLOCKS):
            routes[b] = dout[b, :, 1024:].astype(F32).T[:8, :]

    for n in range(1, NX):

        @pl.when(j == n - 1)
        def _(n=n):
            for copy in weight_copies(n):
                copy.start()

    def wait():
        for n in range(NX):

            @pl.when(j == n)
            def _(n=n):
                for copy in weight_copies(n):
                    copy.wait()

    mine = pl.ds(pl.multiple_of(j * MOST, MOST), MOST)

    def put(ref):
        def put_rows(at, values):
            for b in range(BLOCKS):
                ref[b, mine, at] = values[b * MOST : (b + 1) * MOST, :]

        return put_rows

    expert = (y * NX + j) * NC + c
    found = find_rows(routes, expert)
    for b in range(BLOCKS):
        picks[b, mine, :] = found[b]
    slot = lax.rem(j, 2)
    one_expert(
        found, expert, second, dout, wr_ref, gu_w.at[slot], dn_w.at[slot], wait,
        rows, grads, pre, hidden, dy, both, logit_grad, put(results), put(backs), gw_ref, gwr_ref,
    )

    @pl.when(j == NX - 1)
    def _():
        sent = []
        for src, dsts in ((backs, (back0, back1)), (results, (res0, res1))):
            for b in reversed(range(BLOCKS)):
                turn = len(sent)
                if turn >= 2:
                    sent[turn - 2].wait()
                stage[turn % 2] = mm_tn(picks[b], src[b]).astype(BF)
                to = dsts[b // NY].at[lax.rem(b % NY - y + NY, NY)]
                copy = pltpu.make_async_copy(stage.at[turn % 2], to, out_sems.at[turn % 2])
                copy.start()
                sent.append(copy)
        sent[-2].wait()
        sent[-1].wait()


def experts_step(place, w_rout, weights, second0, second1, dout0, dout1):
    hbm = pl.BlockSpec(memory_space=pl.ANY)
    whole = pl.BlockSpec((1024, 128), lambda j, place: (0, 0))
    by_x = lambda j, place: (j, 0, 0, 0)
    return pl.pallas_call(
        experts_kernel,
        out_shape=[shaped((NY, 256, 1024), BF)] * 4
        + [shaped((NX, NZ, 384, 1024), BF), shaped((1024, 128), F32)],
        grid_spec=pltpu.PrefetchScalarGridSpec(
            num_scalar_prefetch=1,
            grid=(NX,),
            in_specs=[whole] + [hbm] * 5,
            out_specs=[hbm] * 4 + [pl.BlockSpec((1, NZ, 384, 1024), by_x), whole],
            scratch_shapes=[
                pltpu.VMEM((BLOCKS, 256, 1024), BF), pltpu.VMEM((BLOCKS, 256, 1152), BF),
                pltpu.VMEM((2, 1024, 1024), BF), pltpu.VMEM((2, 512, 1024), BF), pltpu.VMEM((ROWS, 1024), BF),
                pltpu.VMEM((ROWS, 1024), BF), pltpu.VMEM((ROWS, 1024), F32), pltpu.VMEM((ROWS, 512), BF),
                pltpu.VMEM((ROWS, 1024), BF), pltpu.VMEM((ROWS, 1024), BF), pltpu.VMEM((ROWS, 128), BF),
                pltpu.VMEM((BLOCKS, 8, 256), F32), pltpu.VMEM((BLOCKS, NX * MOST, 256), BF),
                pltpu.VMEM((BLOCKS, NX * MOST, 1024), BF), pltpu.VMEM((BLOCKS, NX * MOST, 1024), BF),
                pltpu.VMEM((2, 256, 1024), BF), pltpu.SemaphoreType.DMA((10,)),
                pltpu.SemaphoreType.DMA((2, 2 * NZ)), pltpu.SemaphoreType.DMA((2,)),
            ],
        ),
        compiler_params=pltpu.CompilerParams(vmem_limit_bytes=VMEM_LIMIT),
        cost_estimate=COST,
    )(place, w_rout, weights, second0, second1, dout0, dout1)


def shift(values, axis, step):
    size = lax.axis_size(axis)
    return lax.ppermute(values, axis, [(i, (i + step) % size) for i in range(size)])


def exchange(values, axis):
    return lax.all_to_all(values, axis, 0, 0)


def to_each(values, count):
    return jnp.broadcast_to(values[None], (count,) + values.shape)


def add_list(parts):
    total = parts[0].astype(F32)
    for part in parts[1:]:
        total = total + part.astype(F32)
    return total


def hold(values):
    return lax.optimization_barrier(values)


def add_up(parts):
    return jnp.sum(parts.astype(F32), axis=0)


def per_device(
    tokens,
    segments,
    positions,
    routes,
    w_query,
    w_key,
    w_value,
    w_output,
    w_router,
    w_gate,
    w_up,
    w_down,
    g_attn,
    g_ffn,
    g_query,
    g_key,
    cotangent,
):
    y, x, c, z = (lax.axis_index(a) for a in ALL)
    peers = NY * NX * NZ
    place = jnp.stack([x, y, z, c]).astype(jnp.int32)

    t1, t3, t2 = (shift(tokens, "z", k) for k in (1, 3, 2))
    packed = jnp.concatenate([jnp.concatenate([w_gate[0], w_up[0]], axis=1), w_down[0]], axis=0)
    weights = lax.all_gather(packed, ("x", "z"), axis=0).reshape(NX, NZ, 384, 1024)
    by_head = [w_query.reshape(8, NZ, 256), w_key.reshape(8, NZ, 128), w_value.reshape(8, NZ, 128)]
    halves = jnp.concatenate([(positions // 32).reshape(2, 128), (positions % 32).reshape(2, 128)])
    halves = jnp.pad(halves.astype(BF), ((0, 4), (0, 0)))[:, None]
    by_head.append(jnp.broadcast_to(halves, (8, NZ, 128)))
    by_head = jnp.concatenate(by_head, axis=2).transpose(1, 0, 2)
    qkv_near = exchange(to_each(by_head, NY * NX).reshape(peers, 8, 640), SAME_CORE).reshape(512, 640)
    rows = jnp.concatenate([cotangent, jnp.pad(routes.astype(BF), ((0, 0), (0, 120)))], axis=1)
    out_router = to_each(jnp.concatenate([w_output, jnp.pad(w_router, ((0, 0), (0, 96)))], axis=1), peers)
    gains = (g_attn[None], jnp.tile(g_query, 2)[None], jnp.tile(g_key, 2)[None])
    d1, d3 = shift(rows, "y", 1), shift(rows, "y", 3)
    blocks, qkv_near, out_router, rows, d1, d3 = hold(([tokens, t1, t2, t3], qkv_near, out_router, rows, d1, d3))
    qkv_far = shift(qkv_near, "c", 1)
    out_near = exchange(out_router, SAME_CORE).reshape(512, 1152)
    d2 = shift(rows, "y", 2)
    outs = attention_forward(place, blocks, qkv_near, qkv_far, *gains)
    mixed, kept = outs[:NZ], outs[NZ:]
    mixed, out_near, d2 = hold((mixed, out_near, d2))
    mixed = [mixed[0]] + [shift(mixed[k], "z", k) for k in range(1, NZ)]
    out_far = shift(out_near, "c", 1)
    dout0 = jnp.stack([rows, d1, d2, d3])
    dout1 = shift(dout0, "c", 1)
    mixed, dout1 = hold((mixed, dout1))
    middle, second, w_out, w_rout = middle_step(place, tokens, mixed, out_near, out_far, g_ffn[None])
    second0 = exchange(second, "y")
    second1 = shift(second0, "c", 1)
    back0, back1, res0, res1, grad_experts, grad_router = experts_step(
        place, w_rout, weights, second0, second1, dout0, dout1
    )
    grad_experts = lax.psum_scatter(
        grad_experts.reshape(NX * NZ, 384, 1024), ("x", "z"), scatter_dimension=0, tiled=True
    )[0]

    back = (back0.astype(F32) + shift(back1, "c", 1).astype(F32)).astype(BF)
    back, res0, res1 = hold((back, res0, res1))
    res1 = shift(res1, "c", 1)
    back = [back[0]] + [shift(back[k], "y", k) for k in range(1, NY)]
    result = [(res0[k].astype(F32) + res1[k].astype(F32)).astype(BF) for k in range(NY)]
    back, result = hold((back, result))
    result = [result[0]] + [shift(result[k], "y", k) for k in range(1, NY)]
    grad_middle, *grad_mixed, da, grad_g_ffn = middle_back(place, back, middle, cotangent, w_out, g_ffn[None])
    grad_mixed, da = hold((grad_mixed, da))
    grad_mixed = [grad_mixed[0]] + [shift(grad_mixed[k], "z", k) for k in range(1, NZ)]
    near, far = output_weight(place, da, mixed, grad_router, grad_g_ffn)
    far = shift(far, "c", 1)
    near = (near.astype(F32) + far.astype(F32)).astype(BF)
    grad_mixed, near = hold((grad_mixed, near))
    dense = exchange(near.reshape(peers, 8, 1280), SAME_CORE)
    *grad_first, near, far = attention_backward(place, grad_mixed, *gains, kept)
    grad_first, near, far, result = hold((grad_first, near, far, result))
    far = shift(far, "c", 1)
    grad_first = [grad_first[0]] + [shift(grad_first[k], "z", k) for k in range(1, NZ)]
    near = (near.astype(F32) + far.astype(F32)).astype(BF)
    late = exchange(near.reshape(peers, 8, 768), SAME_CORE)
    grad_experts = grad_experts.astype(F32)
    output = (middle + add_list(result)).astype(BF)
    dense = add_up(dense)
    grad_g_ffn = dense[:, 1152:].reshape(1024)
    grad_w = add_up(late[:, :, :512].reshape(NY * NX, NZ, 8, 512))
    late = add_up(late[:, :, 512:])
    grad_query = grad_w[:, :, :256].transpose(1, 0, 2).reshape(8, 1024)
    grad_key = grad_w[:, :, 256:384].transpose(1, 0, 2).reshape(8, 512)
    grad_value = grad_w[:, :, 384:].transpose(1, 0, 2).reshape(8, 512)
    grad_heads = late[:3, 128:].reshape(6, HEAD)

    grad_first = add_list(grad_first)
    unit, scale = unit_rows(tokens.astype(F32))
    by_gain = grad_first * g_attn
    grad_tokens = grad_middle + scale * (
        by_gain - unit * jnp.mean(by_gain * unit, axis=-1, keepdims=True)
    )
    return (
        output,
        grad_tokens.astype(BF),
        grad_query,
        grad_key,
        grad_value,
        dense[:, :1024],
        dense[:, 1024 : 1024 + EXPERTS],
        grad_experts[None, :256, :512],
        grad_experts[None, :256, 512:],
        grad_experts[None, 256:],
        late[:, :128].reshape(1024),
        grad_g_ffn,
        grad_heads[:4].sum(axis=0),
        grad_heads[4:].sum(axis=0),
    )


def solution(mesh):
    grid = Mesh(mesh.devices.reshape(NY, NX, NC, NZ), ALL)
    rows = P(ALL, None)
    line = P(ALL)
    expert = P(("y", "x", "c"), "z", None)
    in_specs = (rows, line, line, rows) + (rows,) * 5 + (expert,) * 3 + (P(),) * 4 + (rows,)
    out_specs = (rows,) * 7 + (expert,) * 3 + (P(),) * 4
    return jax.shard_map(
        per_device, mesh=grid, in_specs=in_specs, out_specs=out_specs, check_vma=False
    )
```

```python
import math
from functools import partial

import jax
import jax.numpy as jnp
from jax import lax
from jax.experimental import pallas as pl
from jax.experimental.pallas import tpu as pltpu
from jax.sharding import Mesh, PartitionSpec as P

HEAD = 64
EXPERTS = 32
MOST = 96
EPS = 1e-06
NEG = -1e30
NY, NX, NC, NZ = 4, 4, 2, 4
ALL = ("y", "x", "c", "z")
SAME_CORE = ("y", "x", "z")
BLOCKS = NY * NC
ROWS = BLOCKS * MOST
BF = jnp.bfloat16
F32 = jnp.float32
VMEM_LIMIT = 60 * 1024 * 1024
COST = pl.CostEstimate(flops=1000, bytes_accessed=1000, transcendentals=0)
LONG = pl.CostEstimate(flops=30_000_000_000, bytes_accessed=80_000_000, transcendentals=0)


def mm(a, b):
    return jnp.dot(a, b, preferred_element_type=F32)


def mm_nt(a, b):
    return lax.dot_general(a, b, (((1,), (1,)), ((), ())), preferred_element_type=F32)


def mm_tn(a, b):
    return lax.dot_general(a, b, (((0,), (0,)), ((), ())), preferred_element_type=F32)


def call(body, out_shape, place, *args, scratch=(), cost=None):
    whole = pl.BlockSpec(memory_space=pltpu.VMEM)
    return pl.pallas_call(
        body,
        out_shape=out_shape,
        in_specs=[pl.BlockSpec(memory_space=pltpu.SMEM)] + [whole] * len(args),
        out_specs=[whole] * len(out_shape),
        scratch_shapes=list(scratch),
        compiler_params=pltpu.CompilerParams(vmem_limit_bytes=VMEM_LIMIT),
        cost_estimate=cost,
    )(place, *args)


def shaped(shape, dtype):
    return jax.ShapeDtypeStruct(shape, dtype)


def halves_swapped(values):
    width = values.shape[1]
    lane = lax.broadcasted_iota(jnp.int32, values.shape, 1)
    low = (lane % HEAD) < (HEAD // 2)
    return jnp.where(
        low, pltpu.roll(values, width - HEAD // 2, 1), pltpu.roll(values, HEAD // 2, 1)
    )


def head_mean(values):
    width = values.shape[1]
    row = lax.broadcasted_iota(jnp.int32, (width, width), 0) // HEAD
    col = lax.broadcasted_iota(jnp.int32, (width, width), 1) // HEAD
    ones = jnp.where(row == col, 1.0 / HEAD, 0.0).astype(BF)
    high = values.astype(BF)
    rest = (values - high.astype(F32)).astype(BF)
    return mm(high, ones) + mm(rest, ones)


def unit_rows(values):
    scale = lax.rsqrt(jnp.mean(values * values, axis=-1, keepdims=True) + EPS)
    return values * scale, scale


def wide(values, width):
    return jnp.concatenate([values] * (width // values.shape[1]), axis=1)


def block_rows(place):
    return pl.ds(pl.multiple_of(lax.rem(place + NZ, NZ) * 256, 256), 256)


def both_cores(to_ref, near_ref, far_ref, c, width):
    for n in range(NY * NX):
        for src, core in ((near_ref, c), (far_ref, 1 - c)):
            to_ref[pl.ds(pl.multiple_of(n * 64 + core * 32, 32), 32), :] = src[n * 32 : (n + 1) * 32, :width]


def each_core(near_ref, far_ref, src_ref, c):
    for n in range(NY * NX):
        for dst, core in ((near_ref, c), (far_ref, 1 - c)):
            dst[n * 32 : (n + 1) * 32, :] = src_ref[pl.ds(pl.multiple_of(n * 64 + core * 32, 32), 32), :]


def for_each(values):
    width = values.shape[1]
    rows = [values[:, k * 128 : (k + 1) * 128] for k in range(width // 128)]
    rows = rows + [jnp.zeros((1, 128), F32)] * (8 - len(rows))
    rows = jnp.concatenate(rows, axis=0)
    return jnp.broadcast_to(rows[None], (128, 8, 128)).reshape(1024, 128).astype(BF)


def key_mask(positions_ref, i):
    keys = (i + 1) * 256
    key = lax.broadcasted_iota(jnp.int32, (keys, 256), 0)
    query = i * 256 + lax.broadcasted_iota(jnp.int32, (1, 256), 1)
    first = query - positions_ref[:, i * 256 : (i + 1) * 256]
    return (key >= first) & (key <= query)


def attention_forward_kernel(
    place_ref, t0, t1, t2, t3, near_ref, far_ref, ga_ref, gq_ref, gk_ref,
    m0, m1, m2, m3, seq_ref, w_ref, pos_ref, cos_ref, sin_ref, raw_ref, q_ref, k_ref, v_ref, lse_ref,
    vt_ref, mixed_ref,
):
    z, c = place_ref[2], place_ref[3]
    both_cores(w_ref, near_ref, far_ref, c, 512)
    at = (place_ref[1] * NX + place_ref[0]) * 32
    packed = near_ref[pl.ds(pl.multiple_of(at, 32), 32), 512:].astype(F32)
    packed = [packed[8 * k + r : 8 * k + r + 1] * 32.0 + packed[8 * k + r + 2 : 8 * k + r + 3] for k in range(NZ) for r in range(2)]
    position = jnp.concatenate(packed, axis=1)
    pos_ref[...] = position.astype(jnp.int32)
    step = lax.broadcasted_iota(jnp.int32, (HEAD // 2, 1024), 0).astype(F32)
    angle = jnp.exp(step * (-2.0 * math.log(10000.0) / HEAD)) * position
    cos, sin = jnp.cos(angle).T, jnp.sin(angle).T
    cos_ref[...] = jnp.concatenate([cos] * 4, axis=1)
    sin_ref[...] = jnp.concatenate([-sin, sin] * 2, axis=1)
    for k, tokens_ref in enumerate((t0, t1, t2, t3)):
        seq_ref[block_rows(z - k), :] = tokens_ref[...]

    def project(i, _):
        rows = pl.ds(pl.multiple_of(i * 256, 256), 256)
        unit, _ = unit_rows(seq_ref[rows, :].astype(F32))
        raw = mm((unit * ga_ref[...]).astype(BF), w_ref[...])
        raw_ref[rows, :] = raw[:, :384]
        cos, sin = cos_ref[rows, :], sin_ref[rows, :]
        for width, start, gain_ref, out_ref in ((256, 0, gq_ref, q_ref), (128, 256, gk_ref, k_ref)):
            part = raw[:, start : start + width]
            part = part * lax.rsqrt(head_mean(part * part) + EPS) * wide(gain_ref[...], width)
            part = part * wide(cos, width) + halves_swapped(part) * wide(sin, width)
            part = part.astype(BF)
            for h in range(width // HEAD):
                out_ref[h, rows, :] = part[:, h * HEAD : (h + 1) * HEAD]
        values = raw[:, 384:].astype(BF)
        for h in range(2):
            v_ref[h, rows, :] = values[:, h * HEAD : (h + 1) * HEAD]
        vt_ref[:, rows] = values.astype(F32).T.astype(BF)
        return 0

    lax.fori_loop(0, 4, project, 0)
    for i in range(4):
        keys = (i + 1) * 256
        allowed = key_mask(pos_ref, i)

        def pair(g, _, i=i, keys=keys, allowed=allowed):
            outs = []
            for s in range(2):
                scores = mm_nt(k_ref[g, :keys, :], q_ref[2 * g + s, i * 256 : keys, :]) * HEAD**-0.5
                scores = jnp.where(allowed, scores, NEG)
                top = jnp.max(scores, axis=0, keepdims=True)
                probs = jnp.exp(scores - top)
                total = jnp.sum(probs, axis=0, keepdims=True)
                lse_ref[2 * g + s, :, i * 256 : keys] = top + jnp.log(total)
                at = pl.ds(pl.multiple_of(g * HEAD, HEAD), HEAD)
                outs.append(mm(vt_ref[at, :keys], probs.astype(BF)) / total)
            both = jnp.concatenate(outs, axis=0).T
            mixed_ref[i * 256 : keys, pl.ds(pl.multiple_of(g * 128, 128), 128)] = both.astype(BF)
            return 0

        lax.fori_loop(0, 2, pair, 0)
    for k, out_ref in enumerate((m0, m1, m2, m3)):
        out_ref[...] = mixed_ref[block_rows(z + k), :]


def attention_forward(place, tokens, near, far, g_attn, g_query, g_key):
    return call(
        attention_forward_kernel,
        [shaped((256, 256), BF)] * NZ + [
            shaped((1024, 1024), BF), shaped((1024, 512), BF), shaped((1, 1024), jnp.int32),
            shaped((1024, 128), F32), shaped((1024, 128), F32), shaped((1024, 384), F32), shaped((4, 1024, HEAD), BF),
            shaped((2, 1024, HEAD), BF), shaped((2, 1024, HEAD), BF), shaped((4, 1, 1024), F32),
        ],
        place, *tokens, near, far, g_attn, g_query, g_key,
        scratch=[pltpu.VMEM((128, 1024), BF), pltpu.VMEM((1024, 256), BF)],
        cost=COST,
    )


def attention_backward_kernel(
    place_ref, gm0, gm1, gm2, gm3, ga_ref, gq_ref, gk_ref, da_ref, x0, x1, x2, x3, router_ref, ffn_ref,
    seq_ref, w_ref, pos_ref, cos_ref, sin_ref, raw_ref, q_ref, k_ref, v_ref, lse_ref,
    p0, p1, p2, p3, near_ref, far_ref,
    gw_ref, kt_ref, do_ref, dq_ref, dk_ref, dv_ref, first_ref, graw_ref, gains_ref, heads_ref,
):
    z = place_ref[2]
    for h in range(4):
        for k, gm_ref in enumerate((gm0, gm1, gm2, gm3)):
            do_ref[h, block_rows(z - k), :] = gm_ref[:, h * HEAD : (h + 1) * HEAD]
    for g in range(2):
        kt_ref[g] = k_ref[g].astype(F32).T.astype(BF)
        dk_ref[g] = jnp.zeros((1024, HEAD), F32)
        dv_ref[g] = jnp.zeros((1024, HEAD), F32)
    for i in range(4):
        keys = (i + 1) * 256
        rows = slice(i * 256, keys)
        allowed = key_mask(pos_ref, i)

        def pair(g, _, keys=keys, rows=rows, allowed=allowed):
            grads = []
            dk = jnp.zeros((keys, HEAD), F32)
            dv = jnp.zeros((keys, HEAD), F32)
            for s in range(2):
                h = 2 * g + s
                query, dout = q_ref[h, rows, :], do_ref[h, rows, :]
                scores = mm_nt(k_ref[g, :keys, :], query) * HEAD**-0.5
                probs = jnp.where(allowed, jnp.exp(scores - lse_ref[h, :, rows]), 0.0)
                grad_probs = mm_nt(v_ref[g, :keys, :], dout)
                delta = jnp.sum(probs * grad_probs, axis=0, keepdims=True)
                grad_scores = (probs * (grad_probs - delta)).astype(BF)
                dv = dv + mm(probs.astype(BF), dout)
                dk = dk + mm(grad_scores, query)
                grads.append(mm(kt_ref[g, :, :keys], grad_scores) * HEAD**-0.5)
            dk_ref[g, :keys, :] += dk
            dv_ref[g, :keys, :] += dv
            both = jnp.concatenate(grads, axis=0).T
            dq_ref[rows, pl.ds(pl.multiple_of(g * 128, 128), 128)] = both
            return 0

        lax.fori_loop(0, 2, pair, 0)

    heads_ref[...] = jnp.zeros((1, 384), F32)

    for k, part_ref in enumerate((p0, p1, p2, p3)):
        rows = block_rows(z + k)
        cos, sin = cos_ref[rows, :], sin_ref[rows, :]
        dk = jnp.concatenate([dk_ref[0, rows, :], dk_ref[1, rows, :]], axis=1) * HEAD**-0.5
        dv = jnp.concatenate([dv_ref[0, rows, :], dv_ref[1, rows, :]], axis=1)
        for width, start, gain_ref, grad in (
            (256, 0, gq_ref, dq_ref[rows, :]),
            (128, 256, gk_ref, dk),
        ):
            grad = grad.astype(BF).astype(F32)
            grad = grad * wide(cos, width) - halves_swapped(grad) * wide(sin, width)
            part = raw_ref[rows, start : start + width]
            scale = lax.rsqrt(head_mean(part * part) + EPS)
            part = part * scale
            heads_ref[:, start : start + width] += jnp.sum(grad * part, axis=0, keepdims=True)
            grad = grad * wide(gain_ref[...], width)
            grad = scale * (grad - part * head_mean(grad * part))
            graw_ref[rows, start : start + width] = grad.astype(BF)
        graw_ref[rows, 384:] = dv.astype(BF)
        unit, _ = unit_rows(seq_ref[rows, :].astype(F32))
        first_ref[rows, :] = (unit * ga_ref[...]).astype(BF)
        part_ref[...] = graw_ref[rows, :]

    for i in range(4):
        rows = slice(i * 256, (i + 1) * 256)
        grad = mm_tn(first_ref[:, rows], graw_ref[...])
        gw_ref[rows, :512] = grad.astype(BF)
        total = jnp.sum(grad * w_ref[rows, :].astype(F32), axis=1, keepdims=True)
        gains_ref[:, rows] = jnp.broadcast_to(total, (256, 128)).T[:1, :] / ga_ref[:, rows]
    gw_ref[:, 512:640] = for_each(gains_ref[...])
    gw_ref[:, 640:768] = for_each(heads_ref[...])
    for k, mixed_ref in enumerate((x0, x1, x2, x3)):
        gw_ref[block_rows(z - k), 768:1792] = mm_tn(mixed_ref[...], da_ref[...]).astype(BF)
    gw_ref[:, 1792:1920] = router_ref[...].astype(BF)
    gw_ref[:, 1920:] = for_each(ffn_ref[...])
    each_core(near_ref, far_ref, gw_ref, place_ref[3])


def attention_backward(place, grad_mixed, g_attn, g_query, g_key, da, mixed, grad_router, gain, kept):
    return call(
        attention_backward_kernel,
        [shaped((256, 512), BF)] * NZ + [shaped((512, 2048), BF)] * 2,
        place, *grad_mixed, g_attn, g_query, g_key, da, *mixed, grad_router, gain, *kept,
        scratch=[
            pltpu.VMEM((1024, 2048), BF),
            pltpu.VMEM((2, HEAD, 1024), BF), pltpu.VMEM((4, 1024, HEAD), BF), pltpu.VMEM((1024, 256), F32),
            pltpu.VMEM((2, 1024, HEAD), F32), pltpu.VMEM((2, 1024, HEAD), F32), pltpu.VMEM((1024, 1024), BF),
            pltpu.VMEM((1024, 512), BF), pltpu.VMEM((1, 1024), F32), pltpu.VMEM((1, 384), F32),
        ],
        cost=COST,
    )


def middle_kernel(
    place_ref, tokens_ref, m0, m1, m2, m3, near_ref, far_ref, g_ref,
    middle_ref, second_ref, w_ref, router_ref, all_ref,
):
    z = place_ref[2]
    both_cores(all_ref, near_ref, far_ref, place_ref[3], 1152)
    w_ref[...] = all_ref[:, :1024]
    router_ref[...] = all_ref[:, 1024:]
    total = tokens_ref[...].astype(F32)
    for k, mixed_ref in enumerate((m0, m1, m2, m3)):
        total = total + mm(mixed_ref[...], w_ref[block_rows(z - k), :])
    middle_ref[...] = total
    unit, _ = unit_rows(total)
    second = (unit * g_ref[...]).astype(BF)
    for k in range(NY):
        second_ref[k] = second


def middle_step(place, tokens, mixed, near, far, g_ffn):
    return call(
        middle_kernel,
        [
            shaped((256, 1024), F32), shaped((NY, 256, 1024), BF), shaped((1024, 1024), BF),
            shaped((1024, 128), BF),
        ],
        place, tokens, *mixed, near, far, g_ffn,
        scratch=[pltpu.VMEM((1024, 1152), BF)],
        cost=COST,
    )


def middle_back_kernel(
    place_ref, back_ref, middle_ref, dout_ref, w_ref, g_ref,
    grad_ref, gm0, gm1, gm2, gm3, da_ref, gain_ref,
):
    z = place_ref[2]
    grad = back_ref[0].astype(F32)
    for k in range(1, NY):
        grad = grad + back_ref[k].astype(F32)
    unit, scale = unit_rows(middle_ref[...])
    gain_ref[...] = jnp.sum(grad * unit, axis=0, keepdims=True)
    grad = grad * g_ref[...]
    grad = dout_ref[...].astype(F32) + scale * (grad - unit * jnp.mean(grad * unit, axis=-1, keepdims=True))
    grad_ref[...] = grad
    da_ref[...] = grad.astype(BF)
    for k, gm_ref in enumerate((gm0, gm1, gm2, gm3)):
        gm_ref[...] = mm_nt(da_ref[...], w_ref[block_rows(z + k), :]).astype(BF)


def middle_back(place, back, middle, dout, w_out, g_ffn):
    return call(
        middle_back_kernel,
        [
            shaped((256, 1024), F32), *[shaped((256, 256), BF)] * NZ, shaped((256, 1024), BF),
            shaped((1, 1024), F32),
        ],
        place, back, middle, dout, w_out, g_ffn,
        cost=COST,
    )


def last_kernel(
    place_ref, p0, p1, p2, p3, w_ref, tokens_ref, grad_ref, g_ref, experts_ref, late_ref,
    gt_ref, gate_ref, up_ref, down_ref, q_ref, k_ref, v_ref, o_ref, r_ref, ga_ref, gf_ref, gq_ref, gk_ref,
):
    z = place_ref[2]
    grad = jnp.zeros((256, 1024), F32)
    for k, part_ref in enumerate((p0, p1, p2, p3)):
        grad = grad + mm_nt(part_ref[...], w_ref[lax.rem(z - k + NZ, NZ)])
    unit, scale = unit_rows(tokens_ref[...].astype(F32))
    grad = grad * g_ref[...]
    grad = grad_ref[...] + scale * (grad - unit * jnp.mean(grad * unit, axis=-1, keepdims=True))
    gt_ref[...] = grad.astype(BF)
    gate_ref[0] = experts_ref[:256, :512].astype(F32)
    up_ref[0] = experts_ref[:256, 512:].astype(F32)
    down_ref[0] = experts_ref[256:, :].astype(F32)
    rest = jnp.zeros((8, 1536), F32)
    for q in range(NZ):
        total = jnp.zeros((8, 512), F32)
        for n in range(NY * NX):
            part = late_ref[n * NZ + q].astype(F32)
            total = total + part[:, :512]
            rest = rest + part[:, 512:]
        q_ref[:, q * 256 : (q + 1) * 256] = total[:, :256]
        k_ref[:, q * 128 : (q + 1) * 128] = total[:, 256:384]
        v_ref[:, q * 128 : (q + 1) * 128] = total[:, 384:]
    o_ref[...] = rest[:, 256:1280]
    r_ref[...] = rest[:, 1280 : 1280 + EXPERTS]
    ga_ref[...] = jnp.concatenate([rest[r : r + 1, :128] for r in range(8)], axis=1)
    gf_ref[...] = jnp.concatenate([rest[r : r + 1, 1408:] for r in range(8)], axis=1)
    heads = [rest[r : r + 1, 128 + h * HEAD : 128 + (h + 1) * HEAD] for r in range(3) for h in range(2)]
    gq_ref[...] = heads[0] + heads[1] + heads[2] + heads[3]
    gk_ref[...] = heads[4] + heads[5]


def last_step(place, parts, w_all, tokens, grad_middle, g_attn, grad_experts, late):
    return call(
        last_kernel,
        [
            shaped((256, 1024), BF), *[shaped((1, 256, 512), F32)] * 2, shaped((1, 128, 1024), F32),
            shaped((8, 1024), F32), shaped((8, 512), F32), shaped((8, 512), F32), shaped((8, 1024), F32),
            shaped((8, EXPERTS), F32), shaped((1, 1024), F32), shaped((1, 1024), F32), shaped((1, HEAD), F32),
            shaped((1, HEAD), F32),
        ],
        place, *parts, w_all, tokens, grad_middle, g_attn, grad_experts, late,
        cost=COST,
    )


def find_rows(routes, expert):
    hits = [
        jnp.sum(jnp.where(routes[b] == expert.astype(F32), 1.0, 0.0), axis=0, keepdims=True)
        for b in range(BLOCKS)
    ]
    hits = jnp.concatenate(hits, axis=0)
    row = lax.broadcasted_iota(jnp.int32, (256, 256), 0)
    before = jnp.where(row < lax.broadcasted_iota(jnp.int32, (256, 256), 1), 1.0, 0.0).astype(BF)
    rank = mm(hits.astype(BF), before)
    slots = lax.broadcasted_iota(jnp.int32, (MOST, 256), 0).astype(F32)
    return [
        jnp.where((rank[b : b + 1, :] == slots) & (hits[b : b + 1, :] > 0.5), 1.0, 0.0).astype(BF)
        for b in range(BLOCKS)
    ]


def experts_kernel(
    place_ref, wr_ref, w_ref, s0_ref, s1_ref, d0_ref, d1_ref,
    back0, back1, res0, res1, gw_ref, gwr_ref,
    second, dout, named, gu_w, dn_w, rows, grads, pre, hidden, dy, both, routes, picks, backs, results, router, mine_router,
    logit_grads, stage,
    in_sems, w_sems, out_sems,
):
    j = pl.program_id(0)
    y, c = place_ref[1], place_ref[3]

    def weight_copies(n):
        slot = n % 2
        copies = []
        for q in range(NZ):
            gu, dn = w_ref.at[n, q, pl.ds(0, 256)], w_ref.at[n, q, pl.ds(256, 128)]
            copies.append(pltpu.make_async_copy(gu, gu_w.at[slot, pl.ds(q * 256, 256)], w_sems.at[slot, q]))
            copies.append(pltpu.make_async_copy(dn, dn_w.at[slot, pl.ds(q * 128, 128)], w_sems.at[slot, NZ + q]))
        return copies

    name_copies, second_copies, dout_copies = [], [], []
    for n in range(BLOCKS):
        to = (n // NY) * NY + lax.rem(y - n % NY + NY, NY)
        src = (d0_ref, d1_ref)[n // NY].at[n % NY]
        name_copies.append(pltpu.make_async_copy(src.at[:, pl.ds(1024, 128)], named.at[to], in_sems.at[0, n]))
        dout_copies.append(pltpu.make_async_copy(src.at[:, pl.ds(0, 1024)], dout.at[to], in_sems.at[1, n]))
        src = (s0_ref, s1_ref)[n // NY].at[n % NY]
        second_copies.append(pltpu.make_async_copy(src, second.at[n], in_sems.at[2, n]))

    @pl.when(j == 0)
    def _():
        for copy in name_copies + second_copies + dout_copies + weight_copies(0):
            copy.start()
        for copy in name_copies:
            copy.wait()
        lane = lax.broadcasted_iota(jnp.int32, (256, 128), 1)
        for b in range(BLOCKS):
            routes[b] = named[b].astype(F32).T[:8, :]
        for b in range(BLOCKS):
            second_copies[b].wait()
            logits = jnp.where(lane < EXPERTS, mm(second[b], wr_ref[...]), NEG)
            probs = jnp.exp(logits - jnp.max(logits, axis=-1, keepdims=True))
            probs = probs / jnp.sum(probs, axis=-1, keepdims=True)
            high = probs.astype(BF)
            router[b, :, :128] = high
            router[b, :, 128:] = (probs - high.astype(F32)).astype(BF)
        for copy in dout_copies:
            copy.wait()

    for n in range(1, NX):

        @pl.when(j == n - 1)
        def _(n=n):
            for copy in weight_copies(n):
                copy.start()

    expert = (y * NX + j) * NC + c
    mine = pl.ds(pl.multiple_of(j * MOST, MOST), MOST)
    found = find_rows(routes, expert)
    for b in range(BLOCKS):
        at = slice(b * MOST, (b + 1) * MOST)
        picks[b, mine, :] = found[b]
        rows[at, :] = mm(found[b], second[b]).astype(BF)
        grads[at, :] = mm(found[b], dout[b]).astype(BF)
        probs = mm(found[b], router[b])
        mine_router[at, :] = probs[:, :128] + probs[:, 128:]
    lane = lax.broadcasted_iota(jnp.int32, (ROWS, 128), 1)
    here = jnp.where(lane == expert, 1.0, 0.0)
    gate = jnp.sum(mine_router[...] * here, axis=-1, keepdims=True)
    for n in range(NX):

        @pl.when(j == n)
        def _(n=n):
            for copy in weight_copies(n):
                copy.wait()

    slot = lax.rem(j, 2)
    gu, dn = gu_w.at[slot], dn_w.at[slot]
    for f in range(2):
        g_at, u_at = slice(f * 256, (f + 1) * 256), slice(512 + f * 256, 768 + f * 256)
        gate_pre = mm(rows[...], gu[:, g_at])
        up_pre = mm(rows[...], gu[:, u_at])
        pre[:, g_at] = gate_pre
        pre[:, u_at] = up_pre
        hidden[:, g_at] = (gate_pre * jax.nn.sigmoid(gate_pre) * up_pre).astype(BF)
    grad_gate = jnp.zeros((ROWS, 1), F32)
    for d in range(4):
        at = slice(d * 256, (d + 1) * 256)
        out = mm(hidden[...], dn[:, at]).astype(BF).astype(F32)
        grad = grads[:, at].astype(F32)
        grad_gate = grad_gate + jnp.sum(out * grad, axis=-1, keepdims=True)
        result = (out * gate).astype(BF)
        for b in range(BLOCKS):
            results[b, mine, at] = result[b * MOST : (b + 1) * MOST, :]
        dy[:, at] = (grad * gate).astype(BF)
    logit_grad = (mine_router[...] * (here - gate) * grad_gate).astype(BF)
    for b in range(BLOCKS):
        logit_grads[b, mine, :] = logit_grad[b * MOST : (b + 1) * MOST, :]
    for f in range(2):
        g_at, u_at = slice(f * 256, (f + 1) * 256), slice(512 + f * 256, 768 + f * 256)
        grad_hidden = mm_nt(dy[...], dn[g_at, :]).astype(BF).astype(F32)
        gate_pre, up_pre = pre[:, g_at], pre[:, u_at]
        sig = jax.nn.sigmoid(gate_pre)
        both[:, g_at] = (grad_hidden * up_pre * sig * (1.0 + gate_pre * (1.0 - sig))).astype(BF)
        both[:, u_at] = (grad_hidden * (gate_pre * sig)).astype(BF)
    for d in range(4):
        at = slice(d * 256, (d + 1) * 256)
        back = mm_nt(both[...], gu[at, :]).astype(BF)
        for b in range(BLOCKS):
            backs[b, mine, at] = back[b * MOST : (b + 1) * MOST, :]
        gw_ref[0, d, :256, :] = mm_tn(rows[:, at], both[...]).astype(BF)
    for f in range(2):
        grad = mm_tn(hidden[:, f * 256 : (f + 1) * 256], dy[...]).astype(BF)
        gw_ref[0, 2 * f, 256:, :] = grad[:128]
        gw_ref[0, 2 * f + 1, 256:, :] = grad[128:]

    @pl.when(j == NX - 1)
    def _():
        sent = []

        def send(values, to):
            turn = len(sent)
            if turn >= 2:
                sent[turn - 2].wait()
            stage[turn % 2] = values.astype(BF)
            copy = pltpu.make_async_copy(stage.at[turn % 2], to, out_sems.at[turn % 2])
            copy.start()
            sent.append(copy)

        grad_router = jnp.zeros((1024, 128), F32)
        for b in reversed(range(BLOCKS)):
            dl = mm_tn(picks[b], logit_grads[b]).astype(BF)
            grad_router = grad_router + mm_tn(second[b], dl)
            back = mm_tn(picks[b], backs[b]) + mm_nt(dl, wr_ref[...])
            send(back, (back0, back1)[b // NY].at[b % NY])
        gwr_ref[...] = grad_router
        for b in reversed(range(BLOCKS)):
            send(mm_tn(picks[b], results[b]), (res0, res1)[b // NY].at[b % NY])
        sent[-2].wait()
        sent[-1].wait()


def experts_step(place, w_rout, weights, second0, second1, dout0, dout1):
    hbm = pl.BlockSpec(memory_space=pl.ANY)
    whole = pl.BlockSpec((1024, 128), lambda j, place: (0, 0))
    return pl.pallas_call(
        experts_kernel,
        out_shape=[shaped((NY, 256, 1024), BF)] * 4 + [shaped((NX, NZ, 384, 1024), BF), shaped((1024, 128), F32)],
        grid_spec=pltpu.PrefetchScalarGridSpec(
            num_scalar_prefetch=1,
            grid=(NX,),
            in_specs=[whole] + [hbm] * 5,
            out_specs=[hbm] * 4 + [pl.BlockSpec((1, NZ, 384, 1024), lambda j, place: (j, 0, 0, 0)), whole],
            scratch_shapes=[
                pltpu.VMEM((BLOCKS, 256, 1024), BF), pltpu.VMEM((BLOCKS, 256, 1024), BF),
                pltpu.VMEM((BLOCKS, 256, 128), BF), pltpu.VMEM((2, 1024, 1024), BF), pltpu.VMEM((2, 512, 1024), BF),
                pltpu.VMEM((ROWS, 1024), BF), pltpu.VMEM((ROWS, 1024), BF), pltpu.VMEM((ROWS, 1024), F32),
                pltpu.VMEM((ROWS, 512), BF), pltpu.VMEM((ROWS, 1024), BF), pltpu.VMEM((ROWS, 1024), BF),
                pltpu.VMEM((BLOCKS, 8, 256), F32), pltpu.VMEM((BLOCKS, NX * MOST, 256), BF),
                pltpu.VMEM((BLOCKS, NX * MOST, 1024), BF), pltpu.VMEM((BLOCKS, NX * MOST, 1024), BF),
                pltpu.VMEM((BLOCKS, 256, 256), BF),
                pltpu.VMEM((ROWS, 128), F32), pltpu.VMEM((BLOCKS, NX * MOST, 128), BF), pltpu.VMEM((2, 256, 1024), BF),
                pltpu.SemaphoreType.DMA((3, BLOCKS)), pltpu.SemaphoreType.DMA((2, 2 * NZ)),
                pltpu.SemaphoreType.DMA((2,)),
            ],
        ),
        compiler_params=pltpu.CompilerParams(vmem_limit_bytes=VMEM_LIMIT),
        cost_estimate=COST,
    )(place, w_rout, weights, second0, second1, dout0, dout1)


def shift(values, axis, step):
    size = lax.axis_size(axis)
    return lax.ppermute(values, axis, [(i, (i + step) % size) for i in range(size)])


def exchange(values, axis):
    return lax.all_to_all(values, axis, 0, 0)


def to_each(values, count):
    return jnp.broadcast_to(values[None], (count,) + values.shape)


def hold(values):
    return lax.optimization_barrier(values)


def add_up(parts):
    return jnp.sum(parts.astype(F32), axis=0)


def per_device(
    tokens,
    segments,
    positions,
    routes,
    w_query,
    w_key,
    w_value,
    w_output,
    w_router,
    w_gate,
    w_up,
    w_down,
    g_attn,
    g_ffn,
    g_query,
    g_key,
    cotangent,
):
    y, x, c, z = (lax.axis_index(a) for a in ALL)
    peers = NY * NX * NZ
    place = jnp.stack([x, y, z, c]).astype(jnp.int32)

    t1, t3, t2 = (shift(tokens, "z", k) for k in (1, 3, 2))
    packed = jnp.concatenate([jnp.concatenate([w_gate[0], w_up[0]], axis=1), w_down[0]], axis=0)
    weights = lax.all_gather(packed, ("x", "z"), axis=0).reshape(NX, NZ, 384, 1024)
    by_head = [w_query.reshape(8, NZ, 256), w_key.reshape(8, NZ, 128), w_value.reshape(8, NZ, 128)]
    halves = jnp.concatenate([(positions // 32).reshape(2, 128), (positions % 32).reshape(2, 128)])
    halves = jnp.pad(halves.astype(BF), ((0, 4), (0, 0)))[:, None]
    by_head.append(jnp.broadcast_to(halves, (8, NZ, 128)))
    by_head = jnp.concatenate(by_head, axis=2).transpose(1, 0, 2)
    qkv_near = exchange(to_each(by_head, NY * NX).reshape(peers, 8, 640), SAME_CORE).reshape(512, 640)
    rows = jnp.concatenate([cotangent, jnp.pad(routes.astype(BF), ((0, 0), (0, 120)))], axis=1)
    out_router = to_each(jnp.concatenate([w_output, jnp.pad(w_router, ((0, 0), (0, 96)))], axis=1), peers)
    gains = (g_attn[None], jnp.tile(g_query, 2)[None], jnp.tile(g_key, 2)[None])
    d1, d3 = shift(rows, "y", 1), shift(rows, "y", 3)
    blocks, qkv_near, out_router, rows, d1, d3 = hold(([tokens, t1, t2, t3], qkv_near, out_router, rows, d1, d3))
    qkv_far = shift(qkv_near, "c", 1)
    out_near = exchange(out_router, SAME_CORE).reshape(512, 1152)
    d2 = shift(rows, "y", 2)
    outs = attention_forward(place, blocks, qkv_near, qkv_far, *gains)
    mixed, kept = outs[:NZ], outs[NZ:]
    mixed, out_near, d2 = hold((mixed, out_near, d2))
    mixed = [mixed[0]] + [shift(mixed[k], "z", k) for k in range(1, NZ)]
    out_far = shift(out_near, "c", 1)
    dout0 = jnp.stack([rows, d1, d2, d3])
    dout1 = shift(dout0, "c", 1)
    mixed, dout1 = hold((mixed, dout1))
    middle, second, w_out, w_rout = middle_step(place, tokens, mixed, out_near, out_far, g_ffn[None])
    second0 = exchange(second, "y")
    second1 = shift(second0, "c", 1)
    w_all = lax.all_gather(kept[1], "z", axis=0)
    back0, back1, res0, res1, grad_experts, grad_router = experts_step(
        place, w_rout, weights, second0, second1, dout0, dout1
    )
    grad_experts = lax.psum_scatter(
        grad_experts.reshape(NX * NZ, 384, 1024), ("x", "z"), scatter_dimension=0, tiled=True
    )[0]
    back = (back0.astype(F32) + shift(back1, "c", 1).astype(F32)).astype(BF)
    back, res0, res1 = hold((back, res0, res1))
    back = exchange(back, "y")
    result = (res0.astype(F32) + shift(res1, "c", 1).astype(F32)).astype(BF)
    back, result = hold((back, result))
    result = exchange(result, "y")
    grad_middle, *grad_mixed, da, grad_g_ffn = middle_back(place, back, middle, cotangent, w_out, g_ffn[None])
    grad_mixed = [grad_mixed[0]] + [shift(grad_mixed[k], "z", k) for k in range(1, NZ)]
    *parts, near, far = attention_backward(
        place, grad_mixed, *gains, da, mixed, grad_router, grad_g_ffn, kept
    )
    parts, near, far, result = hold((parts, near, far, result))
    far = shift(far, "c", 1)
    parts = [parts[0]] + [shift(parts[k], "z", k) for k in range(1, NZ)]
    near = (near.astype(F32) + far.astype(F32)).astype(BF)
    late = exchange(near.reshape(peers, 8, 2048), SAME_CORE)
    output = (middle + add_up(result)).astype(BF)
    parts, late = hold((parts, late))
    (
        grad_tokens, grad_gate, grad_up, grad_down, grad_query, grad_key, grad_value, grad_output, grad_router,
        *grad_gains,
    ) = last_step(place, parts, w_all, tokens, grad_middle, g_attn[None], grad_experts, late)
    return (
        output,
        grad_tokens,
        grad_query,
        grad_key,
        grad_value,
        grad_output,
        grad_router,
        grad_gate,
        grad_up,
        grad_down,
        *[g[0] for g in grad_gains],
    )


def solution(mesh):
    grid = Mesh(mesh.devices.reshape(NY, NX, NC, NZ), ALL)
    rows = P(ALL, None)
    line = P(ALL)
    expert = P(("y", "x", "c"), "z", None)
    in_specs = (rows, line, line, rows) + (rows,) * 5 + (expert,) * 3 + (P(),) * 4 + (rows,)
    out_specs = (rows,) * 7 + (expert,) * 3 + (P(),) * 4
    return jax.shard_map(
        per_device, mesh=grid, in_specs=in_specs, out_specs=out_specs, check_vma=False
    )
```

```python
import math
from functools import partial

import jax
import jax.numpy as jnp
from jax import lax
from jax.experimental import pallas as pl
from jax.experimental.pallas import tpu as pltpu
from jax.sharding import Mesh, PartitionSpec as P

HEAD = 64
EXPERTS = 32
MOST = 96
EPS = 1e-06
NEG = -1e30
NY, NX, NC, NZ = 4, 4, 2, 4
ALL = ("y", "x", "c", "z")
SAME_CORE = ("y", "x", "z")
BLOCKS = NY * NC
EIGHTH = 0.125
ROWS = BLOCKS * MOST
BF = jnp.bfloat16
F32 = jnp.float32
VMEM_LIMIT = 60 * 1024 * 1024
COST = pl.CostEstimate(flops=1000, bytes_accessed=1000, transcendentals=0)
LONG = pl.CostEstimate(flops=30_000_000_000, bytes_accessed=80_000_000, transcendentals=0)


def mm(a, b):
    return jnp.dot(a, b, preferred_element_type=F32)


def mm_nt(a, b):
    return lax.dot_general(a, b, (((1,), (1,)), ((), ())), preferred_element_type=F32)


def mm_tn(a, b):
    return lax.dot_general(a, b, (((0,), (0,)), ((), ())), preferred_element_type=F32)


def call(body, out_shape, place, *args, scratch=(), cost=None):
    whole = pl.BlockSpec(memory_space=pltpu.VMEM)
    return pl.pallas_call(
        body,
        out_shape=out_shape,
        in_specs=[pl.BlockSpec(memory_space=pltpu.SMEM)] + [whole] * len(args),
        out_specs=[whole] * len(out_shape),
        scratch_shapes=list(scratch),
        compiler_params=pltpu.CompilerParams(vmem_limit_bytes=VMEM_LIMIT),
        cost_estimate=cost,
    )(place, *args)


def shaped(shape, dtype):
    return jax.ShapeDtypeStruct(shape, dtype)


def halves_swapped(values):
    width = values.shape[1]
    lane = lax.broadcasted_iota(jnp.int32, values.shape, 1)
    low = (lane % HEAD) < (HEAD // 2)
    return jnp.where(
        low, pltpu.roll(values, width - HEAD // 2, 1), pltpu.roll(values, HEAD // 2, 1)
    )


def head_mean(values):
    width = values.shape[1]
    row = lax.broadcasted_iota(jnp.int32, (width, width), 0) // HEAD
    col = lax.broadcasted_iota(jnp.int32, (width, width), 1) // HEAD
    ones = jnp.where(row == col, 1.0 / HEAD, 0.0).astype(BF)
    high = values.astype(BF)
    rest = (values - high.astype(F32)).astype(BF)
    return mm(high, ones) + mm(rest, ones)


def unit_rows(values):
    scale = lax.rsqrt(jnp.mean(values * values, axis=-1, keepdims=True) + EPS)
    return values * scale, scale


def wide(values, width):
    return jnp.concatenate([values] * (width // values.shape[1]), axis=1)


def block_rows(place):
    return pl.ds(pl.multiple_of(lax.rem(place + NZ, NZ) * 256, 256), 256)


def both_cores(to_ref, near_ref, far_ref, c, width):
    for n in range(NY * NX):
        for src, core in ((near_ref, c), (far_ref, 1 - c)):
            to_ref[pl.ds(pl.multiple_of(n * 64 + core * 32, 32), 32), :] = src[n * 32 : (n + 1) * 32, :width]


def each_core(near_ref, far_ref, src_ref, c):
    for n in range(NY * NX):
        for dst, core in ((near_ref, c), (far_ref, 1 - c)):
            dst[n * 32 : (n + 1) * 32, :] = src_ref[pl.ds(pl.multiple_of(n * 64 + core * 32, 32), 32), :]


def for_each(values):
    width = values.shape[1]
    rows = [values[:, k * 128 : (k + 1) * 128] for k in range(width // 128)]
    rows = rows + [jnp.zeros((1, 128), F32)] * (8 - len(rows))
    rows = jnp.concatenate(rows, axis=0)
    return jnp.broadcast_to(rows[None], (128, 8, 128)).reshape(1024, 128).astype(BF)


def key_mask(positions_ref, i):
    keys = (i + 1) * 256
    key = lax.broadcasted_iota(jnp.int32, (keys, 256), 0)
    query = i * 256 + lax.broadcasted_iota(jnp.int32, (1, 256), 1)
    first = query - positions_ref[:, i * 256 : (i + 1) * 256]
    return (key >= first) & (key <= query)


def attention_forward_kernel(
    place_ref, t0, t1, t2, t3, near_ref, far_ref, ga_ref, gq_ref, gk_ref,
    m0, m1, m2, m3, seq_ref, w_ref, pos_ref, cos_ref, sin_ref, raw_ref, q_ref, k_ref, v_ref, lse_ref,
    vt_ref, mixed_ref,
):
    z, c = place_ref[2], place_ref[3]
    both_cores(w_ref, near_ref, far_ref, c, 512)
    at = (place_ref[1] * NX + place_ref[0]) * 32
    packed = near_ref[pl.ds(pl.multiple_of(at, 32), 32), 512:].astype(F32)
    packed = [packed[8 * k + r : 8 * k + r + 1] * 32.0 + packed[8 * k + r + 2 : 8 * k + r + 3] for k in range(NZ) for r in range(2)]
    position = jnp.concatenate(packed, axis=1)
    pos_ref[...] = position.astype(jnp.int32)
    step = lax.broadcasted_iota(jnp.int32, (HEAD // 2, 1024), 0).astype(F32)
    angle = jnp.exp(step * (-2.0 * math.log(10000.0) / HEAD)) * position
    cos, sin = jnp.cos(angle).T, jnp.sin(angle).T
    cos_ref[...] = jnp.concatenate([cos] * 4, axis=1)
    sin_ref[...] = jnp.concatenate([-sin, sin] * 2, axis=1)
    for k, tokens_ref in enumerate((t0, t1, t2, t3)):
        seq_ref[block_rows(z - k), :] = tokens_ref[...]

    for i in range(4):
        rows = slice(i * 256, (i + 1) * 256)
        unit, _ = unit_rows(seq_ref[rows, :].astype(F32))
        raw = mm((unit * ga_ref[...]).astype(BF), w_ref[...])
        raw_ref[rows, :] = raw[:, :384]
        cos, sin = cos_ref[rows, :], sin_ref[rows, :]
        for width, start, gain_ref, out_ref in ((256, 0, gq_ref, q_ref), (128, 256, gk_ref, k_ref)):
            part = raw[:, start : start + width]
            part = part * lax.rsqrt(head_mean(part * part) + EPS) * wide(gain_ref[...], width)
            part = part * wide(cos, width) + halves_swapped(part) * wide(sin, width)
            part = part.astype(BF)
            for h in range(width // HEAD):
                out_ref[h, rows, :] = part[:, h * HEAD : (h + 1) * HEAD]
        values = raw[:, 384:].astype(BF)
        for h in range(2):
            v_ref[h, rows, :] = values[:, h * HEAD : (h + 1) * HEAD]
        vt_ref[:, rows] = values.astype(F32).T.astype(BF)

    for i in range(4):
        keys = (i + 1) * 256
        allowed = key_mask(pos_ref, i)

        for g in range(2):
            outs = []
            for s in range(2):
                scores = mm_nt(k_ref[g, :keys, :], q_ref[2 * g + s, i * 256 : keys, :] * EIGHTH)
                scores = jnp.where(allowed, scores, NEG)
                top = jnp.max(scores, axis=0, keepdims=True)
                probs = jnp.exp(scores - top)
                total = jnp.sum(probs, axis=0, keepdims=True)
                lse_ref[2 * g + s, :, i * 256 : keys] = top + jnp.log(total)
                at = slice(g * HEAD, (g + 1) * HEAD)
                outs.append(mm(vt_ref[at, :keys], probs.astype(BF)) / total)
            both = jnp.concatenate(outs, axis=0).T
            mixed_ref[i * 256 : keys, slice(g * 128, (g + 1) * 128)] = both.astype(BF)
    for k, out_ref in enumerate((m0, m1, m2, m3)):
        out_ref[...] = mixed_ref[block_rows(z + k), :]


def attention_forward(place, tokens, near, far, g_attn, g_query, g_key):
    return call(
        attention_forward_kernel,
        [shaped((256, 256), BF)] * NZ + [
            shaped((1024, 1024), BF), shaped((1024, 512), BF), shaped((1, 1024), jnp.int32),
            shaped((1024, 128), F32), shaped((1024, 128), F32), shaped((1024, 384), F32), shaped((4, 1024, HEAD), BF),
            shaped((2, 1024, HEAD), BF), shaped((2, 1024, HEAD), BF), shaped((4, 1, 1024), F32),
        ],
        place, *tokens, near, far, g_attn, g_query, g_key,
        scratch=[pltpu.VMEM((128, 1024), BF), pltpu.VMEM((1024, 256), BF)],
        cost=COST,
    )


def attention_backward_kernel(
    place_ref, gm0, gm1, gm2, gm3, ga_ref, gq_ref, gk_ref, da_ref, x0, x1, x2, x3, router_ref, ffn_ref,
    seq_ref, w_ref, pos_ref, cos_ref, sin_ref, raw_ref, q_ref, k_ref, v_ref, lse_ref,
    p0, p1, p2, p3, near_ref, far_ref,
    gw_ref, kt_ref, do_ref, dq_ref, dk_ref, dv_ref, first_ref, graw_ref, gains_ref, heads_ref,
):
    z = place_ref[2]
    for h in range(4):
        for k, gm_ref in enumerate((gm0, gm1, gm2, gm3)):
            do_ref[h, block_rows(z - k), :] = gm_ref[:, h * HEAD : (h + 1) * HEAD]
    for g in range(2):
        kt_ref[g] = k_ref[g].astype(F32).T.astype(BF)
        dk_ref[g] = jnp.zeros((1024, HEAD), F32)
        dv_ref[g] = jnp.zeros((1024, HEAD), F32)
    for i in range(4):
        keys = (i + 1) * 256
        rows = slice(i * 256, keys)
        allowed = key_mask(pos_ref, i)

        for g in range(2):
            grads = []
            dk = jnp.zeros((keys, HEAD), F32)
            dv = jnp.zeros((keys, HEAD), F32)
            for s in range(2):
                h = 2 * g + s
                query, dout = q_ref[h, rows, :], do_ref[h, rows, :]
                scores = mm_nt(k_ref[g, :keys, :], query * EIGHTH)
                probs = jnp.where(allowed, jnp.exp(scores - lse_ref[h, :, rows]), 0.0)
                grad_probs = mm_nt(v_ref[g, :keys, :], dout)
                delta = jnp.sum(probs * grad_probs, axis=0, keepdims=True)
                grad_scores = (probs * (grad_probs - delta)).astype(BF)
                dv = dv + mm(probs.astype(BF), dout)
                dk = dk + mm(grad_scores, query)
                grads.append(mm(kt_ref[g, :, :keys], grad_scores) * HEAD**-0.5)
            dk_ref[g, :keys, :] += dk
            dv_ref[g, :keys, :] += dv
            both = jnp.concatenate(grads, axis=0).T
            dq_ref[rows, slice(g * 128, (g + 1) * 128)] = both

    heads_ref[...] = jnp.zeros((1, 384), F32)

    for k, part_ref in enumerate((p0, p1, p2, p3)):
        rows = block_rows(z + k)
        cos, sin = cos_ref[rows, :], sin_ref[rows, :]
        dk = jnp.concatenate([dk_ref[0, rows, :], dk_ref[1, rows, :]], axis=1) * HEAD**-0.5
        dv = jnp.concatenate([dv_ref[0, rows, :], dv_ref[1, rows, :]], axis=1)
        for width, start, gain_ref, grad in (
            (256, 0, gq_ref, dq_ref[rows, :]),
            (128, 256, gk_ref, dk),
        ):
            grad = grad.astype(BF).astype(F32)
            grad = grad * wide(cos, width) - halves_swapped(grad) * wide(sin, width)
            part = raw_ref[rows, start : start + width]
            scale = lax.rsqrt(head_mean(part * part) + EPS)
            part = part * scale
            heads_ref[:, start : start + width] += jnp.sum(grad * part, axis=0, keepdims=True)
            grad = grad * wide(gain_ref[...], width)
            grad = scale * (grad - part * head_mean(grad * part))
            graw_ref[rows, start : start + width] = grad.astype(BF)
        graw_ref[rows, 384:] = dv.astype(BF)
        unit, _ = unit_rows(seq_ref[rows, :].astype(F32))
        first_ref[rows, :] = (unit * ga_ref[...]).astype(BF)
        part_ref[...] = graw_ref[rows, :]

    for i in range(4):
        rows = slice(i * 256, (i + 1) * 256)
        grad = mm_tn(first_ref[:, rows], graw_ref[...])
        gw_ref[rows, :512] = grad.astype(BF)
        total = jnp.sum(grad * w_ref[rows, :].astype(F32), axis=1, keepdims=True)
        gains_ref[:, rows] = jnp.broadcast_to(total, (256, 128)).T[:1, :] / ga_ref[:, rows]
    gw_ref[:, 512:640] = for_each(gains_ref[...])
    gw_ref[:, 640:768] = for_each(heads_ref[...])
    for k, mixed_ref in enumerate((x0, x1, x2, x3)):
        gw_ref[block_rows(z - k), 768:1792] = mm_tn(mixed_ref[...], da_ref[...]).astype(BF)
    gw_ref[:, 1792:1920] = router_ref[...].astype(BF)
    gw_ref[:, 1920:] = for_each(ffn_ref[...])
    each_core(near_ref, far_ref, gw_ref, place_ref[3])


def attention_backward(place, grad_mixed, g_attn, g_query, g_key, da, mixed, grad_router, gain, kept):
    return call(
        attention_backward_kernel,
        [shaped((256, 512), BF)] * NZ + [shaped((512, 2048), BF)] * 2,
        place, *grad_mixed, g_attn, g_query, g_key, da, *mixed, grad_router, gain, *kept,
        scratch=[
            pltpu.VMEM((1024, 2048), BF),
            pltpu.VMEM((2, HEAD, 1024), BF), pltpu.VMEM((4, 1024, HEAD), BF), pltpu.VMEM((1024, 256), F32),
            pltpu.VMEM((2, 1024, HEAD), F32), pltpu.VMEM((2, 1024, HEAD), F32), pltpu.VMEM((1024, 1024), BF),
            pltpu.VMEM((1024, 512), BF), pltpu.VMEM((1, 1024), F32), pltpu.VMEM((1, 384), F32),
        ],
        cost=COST,
    )


def middle_kernel(
    place_ref, tokens_ref, m0, m1, m2, m3, near_ref, far_ref, g_ref,
    middle_ref, second_ref, w_ref, router_ref, all_ref,
):
    z = place_ref[2]
    both_cores(all_ref, near_ref, far_ref, place_ref[3], 1152)
    w_ref[...] = all_ref[:, :1024]
    router_ref[...] = all_ref[:, 1024:]
    total = tokens_ref[...].astype(F32)
    for k, mixed_ref in enumerate((m0, m1, m2, m3)):
        total = total + mm(mixed_ref[...], w_ref[block_rows(z - k), :])
    middle_ref[...] = total
    unit, _ = unit_rows(total)
    second = (unit * g_ref[...]).astype(BF)
    for k in range(NY):
        second_ref[k] = second


def middle_step(place, tokens, mixed, near, far, g_ffn):
    return call(
        middle_kernel,
        [
            shaped((256, 1024), F32), shaped((NY, 256, 1024), BF), shaped((1024, 1024), BF),
            shaped((1024, 128), BF),
        ],
        place, tokens, *mixed, near, far, g_ffn,
        scratch=[pltpu.VMEM((1024, 1152), BF)],
        cost=COST,
    )


def middle_back_kernel(
    place_ref, back_ref, middle_ref, dout_ref, w_ref, g_ref,
    grad_ref, gm0, gm1, gm2, gm3, da_ref, gain_ref,
):
    z = place_ref[2]
    grad = back_ref[0].astype(F32)
    for k in range(1, NY):
        grad = grad + back_ref[k].astype(F32)
    unit, scale = unit_rows(middle_ref[...])
    gain_ref[...] = jnp.sum(grad * unit, axis=0, keepdims=True)
    grad = grad * g_ref[...]
    grad = dout_ref[...].astype(F32) + scale * (grad - unit * jnp.mean(grad * unit, axis=-1, keepdims=True))
    grad_ref[...] = grad
    da_ref[...] = grad.astype(BF)
    for k, gm_ref in enumerate((gm0, gm1, gm2, gm3)):
        gm_ref[...] = mm_nt(da_ref[...], w_ref[block_rows(z + k), :]).astype(BF)


def middle_back(place, back, middle, dout, w_out, g_ffn):
    return call(
        middle_back_kernel,
        [
            shaped((256, 1024), F32), *[shaped((256, 256), BF)] * NZ, shaped((256, 1024), BF),
            shaped((1, 1024), F32),
        ],
        place, back, middle, dout, w_out, g_ffn,
        cost=COST,
    )


def last_kernel(
    place_ref, p0, p1, p2, p3, w_ref, tokens_ref, grad_ref, g_ref, experts_ref, late_ref,
    gt_ref, gate_ref, up_ref, down_ref, q_ref, k_ref, v_ref, o_ref, r_ref, ga_ref, gf_ref, gq_ref, gk_ref,
):
    z = place_ref[2]
    grad = jnp.zeros((256, 1024), F32)
    for k, part_ref in enumerate((p0, p1, p2, p3)):
        grad = grad + mm_nt(part_ref[...], w_ref[lax.rem(z - k + NZ, NZ)])
    unit, scale = unit_rows(tokens_ref[...].astype(F32))
    grad = grad * g_ref[...]
    grad = grad_ref[...] + scale * (grad - unit * jnp.mean(grad * unit, axis=-1, keepdims=True))
    gt_ref[...] = grad.astype(BF)
    gate_ref[0] = experts_ref[:256, :512].astype(F32)
    up_ref[0] = experts_ref[:256, 512:].astype(F32)
    down_ref[0] = experts_ref[256:, :].astype(F32)
    rest = jnp.zeros((8, 1536), F32)
    for q in range(NZ):
        total = jnp.zeros((8, 512), F32)
        for n in range(NY * NX):
            part = late_ref[n * NZ + q].astype(F32)
            total = total + part[:, :512]
            rest = rest + part[:, 512:]
        q_ref[:, q * 256 : (q + 1) * 256] = total[:, :256]
        k_ref[:, q * 128 : (q + 1) * 128] = total[:, 256:384]
        v_ref[:, q * 128 : (q + 1) * 128] = total[:, 384:]
    o_ref[...] = rest[:, 256:1280]
    r_ref[...] = rest[:, 1280 : 1280 + EXPERTS]
    ga_ref[...] = jnp.concatenate([rest[r : r + 1, :128] for r in range(8)], axis=1)
    gf_ref[...] = jnp.concatenate([rest[r : r + 1, 1408:] for r in range(8)], axis=1)
    heads = [rest[r : r + 1, 128 + h * HEAD : 128 + (h + 1) * HEAD] for r in range(3) for h in range(2)]
    gq_ref[...] = heads[0] + heads[1] + heads[2] + heads[3]
    gk_ref[...] = heads[4] + heads[5]


def last_step(place, parts, w_all, tokens, grad_middle, g_attn, grad_experts, late):
    return call(
        last_kernel,
        [
            shaped((256, 1024), BF), *[shaped((1, 256, 512), F32)] * 2, shaped((1, 128, 1024), F32),
            shaped((8, 1024), F32), shaped((8, 512), F32), shaped((8, 512), F32), shaped((8, 1024), F32),
            shaped((8, EXPERTS), F32), shaped((1, 1024), F32), shaped((1, 1024), F32), shaped((1, HEAD), F32),
            shaped((1, HEAD), F32),
        ],
        place, *parts, w_all, tokens, grad_middle, g_attn, grad_experts, late,
        cost=COST,
    )


def find_rows(routes, expert):
    hits = [
        jnp.sum(jnp.where(routes[b] == expert.astype(F32), 1.0, 0.0), axis=0, keepdims=True)
        for b in range(BLOCKS)
    ]
    hits = jnp.concatenate(hits, axis=0)
    row = lax.broadcasted_iota(jnp.int32, (256, 256), 0)
    before = jnp.where(row < lax.broadcasted_iota(jnp.int32, (256, 256), 1), 1.0, 0.0).astype(BF)
    rank = mm(hits.astype(BF), before)
    slots = lax.broadcasted_iota(jnp.int32, (MOST, 256), 0).astype(F32)
    return [
        jnp.where((rank[b : b + 1, :] == slots) & (hits[b : b + 1, :] > 0.5), 1.0, 0.0).astype(BF)
        for b in range(BLOCKS)
    ]


def experts_kernel(
    place_ref, wr_ref, w_ref, s0_ref, s1_ref, d0_ref, d1_ref,
    back0, back1, res0, res1, gw_ref, gwr_ref,
    second, dout, named, gu_w, dn_w, rows, grads, pre, hidden, dy, both, routes, picks, backs, results, router, mine_router,
    logit_grads, stage,
    in_sems, w_sems, out_sems,
):
    j = pl.program_id(0)
    y, c = place_ref[1], place_ref[3]

    def weight_copies(n):
        slot = n % 2
        copies = []
        for q in range(NZ):
            gu, dn = w_ref.at[n, q, pl.ds(0, 256)], w_ref.at[n, q, pl.ds(256, 128)]
            copies.append(pltpu.make_async_copy(gu, gu_w.at[slot, pl.ds(q * 256, 256)], w_sems.at[slot, q]))
            copies.append(pltpu.make_async_copy(dn, dn_w.at[slot, pl.ds(q * 128, 128)], w_sems.at[slot, NZ + q]))
        return copies

    name_copies, second_copies, dout_copies = [], [], []
    for n in range(BLOCKS):
        to = (n // NY) * NY + lax.rem(y - n % NY + NY, NY)
        src = (d0_ref, d1_ref)[n // NY].at[n % NY]
        name_copies.append(pltpu.make_async_copy(src.at[:, pl.ds(1024, 128)], named.at[to], in_sems.at[0, n]))
        dout_copies.append(pltpu.make_async_copy(src.at[:, pl.ds(0, 1024)], dout.at[to], in_sems.at[1, n]))
        src = (s0_ref, s1_ref)[n // NY].at[n % NY]
        second_copies.append(pltpu.make_async_copy(src, second.at[n], in_sems.at[2, n]))

    @pl.when(j == 0)
    def _():
        for copy in name_copies + second_copies + dout_copies + weight_copies(0):
            copy.start()
        for copy in name_copies:
            copy.wait()
        lane = lax.broadcasted_iota(jnp.int32, (256, 128), 1)
        for b in range(BLOCKS):
            routes[b] = named[b].astype(F32).T[:8, :]
        for b in range(BLOCKS):
            second_copies[b].wait()
            logits = jnp.where(lane < EXPERTS, mm(second[b], wr_ref[...]), NEG)
            probs = jnp.exp(logits - jnp.max(logits, axis=-1, keepdims=True))
            probs = probs / jnp.sum(probs, axis=-1, keepdims=True)
            high = probs.astype(BF)
            router[b, :, :128] = high
            router[b, :, 128:] = (probs - high.astype(F32)).astype(BF)
        for copy in dout_copies:
            copy.wait()

    for n in range(1, NX):

        @pl.when(j == n - 1)
        def _(n=n):
            for copy in weight_copies(n):
                copy.start()

    expert = (y * NX + j) * NC + c
    mine = pl.ds(pl.multiple_of(j * MOST, MOST), MOST)
    found = find_rows(routes, expert)
    for b in range(BLOCKS):
        at = slice(b * MOST, (b + 1) * MOST)
        picks[b, mine, :] = found[b]
        rows[at, :] = mm(found[b], second[b]).astype(BF)
        grads[at, :] = mm(found[b], dout[b]).astype(BF)
        probs = mm(found[b], router[b])
        mine_router[at, :] = probs[:, :128] + probs[:, 128:]
    lane = lax.broadcasted_iota(jnp.int32, (ROWS, 128), 1)
    here = jnp.where(lane == expert, 1.0, 0.0)
    gate = jnp.sum(mine_router[...] * here, axis=-1, keepdims=True)
    for n in range(NX):

        @pl.when(j == n)
        def _(n=n):
            for copy in weight_copies(n):
                copy.wait()

    slot = lax.rem(j, 2)
    gu, dn = gu_w.at[slot], dn_w.at[slot]
    for f in range(2):
        g_at, u_at = slice(f * 256, (f + 1) * 256), slice(512 + f * 256, 768 + f * 256)
        gate_pre = mm(rows[...], gu[:, g_at])
        up_pre = mm(rows[...], gu[:, u_at])
        pre[:, g_at] = gate_pre
        pre[:, u_at] = up_pre
        hidden[:, g_at] = (gate_pre * jax.nn.sigmoid(gate_pre) * up_pre).astype(BF)
    grad_gate = jnp.zeros((ROWS, 1), F32)
    for d in range(4):
        at = slice(d * 256, (d + 1) * 256)
        out = mm(hidden[...], dn[:, at]).astype(BF).astype(F32)
        grad = grads[:, at].astype(F32)
        grad_gate = grad_gate + jnp.sum(out * grad, axis=-1, keepdims=True)
        result = (out * gate).astype(BF)
        for b in range(BLOCKS):
            results[b, mine, at] = result[b * MOST : (b + 1) * MOST, :]
        dy[:, at] = (grad * gate).astype(BF)
    logit_grad = (mine_router[...] * (here - gate) * grad_gate).astype(BF)
    for b in range(BLOCKS):
        logit_grads[b, mine, :] = logit_grad[b * MOST : (b + 1) * MOST, :]
    for f in range(2):
        g_at, u_at = slice(f * 256, (f + 1) * 256), slice(512 + f * 256, 768 + f * 256)
        grad_hidden = mm_nt(dy[...], dn[g_at, :]).astype(BF).astype(F32)
        gate_pre, up_pre = pre[:, g_at], pre[:, u_at]
        sig = jax.nn.sigmoid(gate_pre)
        both[:, g_at] = (grad_hidden * up_pre * sig * (1.0 + gate_pre * (1.0 - sig))).astype(BF)
        both[:, u_at] = (grad_hidden * (gate_pre * sig)).astype(BF)
    for d in range(4):
        at = slice(d * 256, (d + 1) * 256)
        back = mm_nt(both[...], gu[at, :]).astype(BF)
        for b in range(BLOCKS):
            backs[b, mine, at] = back[b * MOST : (b + 1) * MOST, :]
        gw_ref[0, d, :256, :] = mm_tn(rows[:, at], both[...]).astype(BF)
    for f in range(2):
        grad = mm_tn(hidden[:, f * 256 : (f + 1) * 256], dy[...]).astype(BF)
        gw_ref[0, 2 * f, 256:, :] = grad[:128]
        gw_ref[0, 2 * f + 1, 256:, :] = grad[128:]

    @pl.when(j == NX - 1)
    def _():
        sent = []

        def send(values, to):
            turn = len(sent)
            if turn >= 2:
                sent[turn - 2].wait()
            stage[turn % 2] = values.astype(BF)
            copy = pltpu.make_async_copy(stage.at[turn % 2], to, out_sems.at[turn % 2])
            copy.start()
            sent.append(copy)

        grad_router = jnp.zeros((1024, 128), F32)
        for b in reversed(range(BLOCKS)):
            dl = mm_tn(picks[b], logit_grads[b]).astype(BF)
            grad_router = grad_router + mm_tn(second[b], dl)
            back = mm_tn(picks[b], backs[b]) + mm_nt(dl, wr_ref[...])
            send(back, (back0, back1)[b // NY].at[b % NY])
        gwr_ref[...] = grad_router
        for b in reversed(range(BLOCKS)):
            send(mm_tn(picks[b], results[b]), (res0, res1)[b // NY].at[b % NY])
        sent[-2].wait()
        sent[-1].wait()


def experts_step(place, w_rout, weights, second0, second1, dout0, dout1):
    hbm = pl.BlockSpec(memory_space=pl.ANY)
    whole = pl.BlockSpec((1024, 128), lambda j, place: (0, 0))
    return pl.pallas_call(
        experts_kernel,
        out_shape=[shaped((NY, 256, 1024), BF)] * 4 + [shaped((NX, NZ, 384, 1024), BF), shaped((1024, 128), F32)],
        grid_spec=pltpu.PrefetchScalarGridSpec(
            num_scalar_prefetch=1,
            grid=(NX,),
            in_specs=[whole] + [hbm] * 5,
            out_specs=[hbm] * 4 + [pl.BlockSpec((1, NZ, 384, 1024), lambda j, place: (j, 0, 0, 0)), whole],
            scratch_shapes=[
                pltpu.VMEM((BLOCKS, 256, 1024), BF), pltpu.VMEM((BLOCKS, 256, 1024), BF),
                pltpu.VMEM((BLOCKS, 256, 128), BF), pltpu.VMEM((2, 1024, 1024), BF), pltpu.VMEM((2, 512, 1024), BF),
                pltpu.VMEM((ROWS, 1024), BF), pltpu.VMEM((ROWS, 1024), BF), pltpu.VMEM((ROWS, 1024), F32),
                pltpu.VMEM((ROWS, 512), BF), pltpu.VMEM((ROWS, 1024), BF), pltpu.VMEM((ROWS, 1024), BF),
                pltpu.VMEM((BLOCKS, 8, 256), F32), pltpu.VMEM((BLOCKS, NX * MOST, 256), BF),
                pltpu.VMEM((BLOCKS, NX * MOST, 1024), BF), pltpu.VMEM((BLOCKS, NX * MOST, 1024), BF),
                pltpu.VMEM((BLOCKS, 256, 256), BF),
                pltpu.VMEM((ROWS, 128), F32), pltpu.VMEM((BLOCKS, NX * MOST, 128), BF), pltpu.VMEM((2, 256, 1024), BF),
                pltpu.SemaphoreType.DMA((3, BLOCKS)), pltpu.SemaphoreType.DMA((2, 2 * NZ)),
                pltpu.SemaphoreType.DMA((2,)),
            ],
        ),
        compiler_params=pltpu.CompilerParams(vmem_limit_bytes=VMEM_LIMIT),
        cost_estimate=COST,
    )(place, w_rout, weights, second0, second1, dout0, dout1)


def shift(values, axis, step):
    size = lax.axis_size(axis)
    return lax.ppermute(values, axis, [(i, (i + step) % size) for i in range(size)])


def exchange(values, axis):
    return lax.all_to_all(values, axis, 0, 0)


def to_each(values, count):
    return jnp.broadcast_to(values[None], (count,) + values.shape)


def hold(values):
    return lax.optimization_barrier(values)


def add_up(parts):
    return jnp.sum(parts.astype(F32), axis=0)


def per_device(
    tokens,
    segments,
    positions,
    routes,
    w_query,
    w_key,
    w_value,
    w_output,
    w_router,
    w_gate,
    w_up,
    w_down,
    g_attn,
    g_ffn,
    g_query,
    g_key,
    cotangent,
):
    y, x, c, z = (lax.axis_index(a) for a in ALL)
    peers = NY * NX * NZ
    place = jnp.stack([x, y, z, c]).astype(jnp.int32)

    t1, t3, t2 = (shift(tokens, "z", k) for k in (1, 3, 2))
    packed = jnp.concatenate([jnp.concatenate([w_gate[0], w_up[0]], axis=1), w_down[0]], axis=0)
    weights = lax.all_gather(packed, ("x", "z"), axis=0).reshape(NX, NZ, 384, 1024)
    by_head = [w_query.reshape(8, NZ, 256), w_key.reshape(8, NZ, 128), w_value.reshape(8, NZ, 128)]
    halves = jnp.concatenate([(positions // 32).reshape(2, 128), (positions % 32).reshape(2, 128)])
    halves = jnp.pad(halves.astype(BF), ((0, 4), (0, 0)))[:, None]
    by_head.append(jnp.broadcast_to(halves, (8, NZ, 128)))
    by_head = jnp.concatenate(by_head, axis=2).transpose(1, 0, 2)
    qkv_near = exchange(to_each(by_head, NY * NX).reshape(peers, 8, 640), SAME_CORE).reshape(512, 640)
    rows = jnp.concatenate([cotangent, jnp.pad(routes.astype(BF), ((0, 0), (0, 120)))], axis=1)
    out_router = to_each(jnp.concatenate([w_output, jnp.pad(w_router, ((0, 0), (0, 96)))], axis=1), peers)
    gains = (g_attn[None], jnp.tile(g_query, 2)[None], jnp.tile(g_key, 2)[None])
    d1, d3 = shift(rows, "y", 1), shift(rows, "y", 3)
    blocks, qkv_near, out_router, rows, d1, d3 = hold(([tokens, t1, t2, t3], qkv_near, out_router, rows, d1, d3))
    qkv_far = shift(qkv_near, "c", 1)
    out_near = exchange(out_router, SAME_CORE).reshape(512, 1152)
    d2 = shift(rows, "y", 2)
    outs = attention_forward(place, blocks, qkv_near, qkv_far, *gains)
    mixed, kept = outs[:NZ], outs[NZ:]
    mixed, out_near, d2 = hold((mixed, out_near, d2))
    mixed = [mixed[0]] + [shift(mixed[k], "z", k) for k in range(1, NZ)]
    out_far = shift(out_near, "c", 1)
    dout0 = jnp.stack([rows, d1, d2, d3])
    dout1 = shift(dout0, "c", 1)
    mixed, dout1 = hold((mixed, dout1))
    middle, second, w_out, w_rout = middle_step(place, tokens, mixed, out_near, out_far, g_ffn[None])
    second0 = exchange(second, "y")
    second1 = shift(second0, "c", 1)
    w_all = lax.all_gather(kept[1], "z", axis=0)
    back0, back1, res0, res1, grad_experts, grad_router = experts_step(
        place, w_rout, weights, second0, second1, dout0, dout1
    )
    grad_experts = lax.psum_scatter(
        grad_experts.reshape(NX * NZ, 384, 1024), ("x", "z"), scatter_dimension=0, tiled=True
    )[0]
    back = (back0.astype(F32) + shift(back1, "c", 1).astype(F32)).astype(BF)
    back, res0, res1 = hold((back, res0, res1))
    back = exchange(back, "y")
    result = (res0.astype(F32) + shift(res1, "c", 1).astype(F32)).astype(BF)
    back, result = hold((back, result))
    result = exchange(result, "y")
    grad_middle, *grad_mixed, da, grad_g_ffn = middle_back(place, back, middle, cotangent, w_out, g_ffn[None])
    grad_mixed = [grad_mixed[0]] + [shift(grad_mixed[k], "z", k) for k in range(1, NZ)]
    *parts, near, far = attention_backward(
        place, grad_mixed, *gains, da, mixed, grad_router, grad_g_ffn, kept
    )
    parts, near, far, result = hold((parts, near, far, result))
    far = shift(far, "c", 1)
    parts = [parts[0]] + [shift(parts[k], "z", k) for k in range(1, NZ)]
    near = (near.astype(F32) + far.astype(F32)).astype(BF)
    late = exchange(near.reshape(peers, 8, 2048), SAME_CORE)
    output = (middle + add_up(result)).astype(BF)
    parts, late = hold((parts, late))
    (
        grad_tokens, grad_gate, grad_up, grad_down, grad_query, grad_key, grad_value, grad_output, grad_router,
        *grad_gains,
    ) = last_step(place, parts, w_all, tokens, grad_middle, g_attn[None], grad_experts, late)
    return (
        output,
        grad_tokens,
        grad_query,
        grad_key,
        grad_value,
        grad_output,
        grad_router,
        grad_gate,
        grad_up,
        grad_down,
        *[g[0] for g in grad_gains],
    )


def solution(mesh):
    grid = Mesh(mesh.devices.reshape(NY, NX, NC, NZ), ALL)
    rows = P(ALL, None)
    line = P(ALL)
    expert = P(("y", "x", "c"), "z", None)
    in_specs = (rows, line, line, rows) + (rows,) * 5 + (expert,) * 3 + (P(),) * 4 + (rows,)
    out_specs = (rows,) * 7 + (expert,) * 3 + (P(),) * 4
    return jax.shard_map(
        per_device, mesh=grid, in_specs=in_specs, out_specs=out_specs, check_vma=False
    )
```
